512 devices in a mesh: patch: 128 (over x, z, core), chan: 4 (over y).
Axes of the slice: x: 4, y: 4, z: 16, core: 2. Of those that a mesh axis runs over, the one named last changes fastest.
Arguments:
- grid_in: bfloat16 [524288, 227], P(('patch', 'chan')), may hold values from -6 to 6
- mesh_embed: bfloat16 [262144, 512], P(('patch', 'chan')), may hold values from -6 to 6
- w_embed: bfloat16 [227, 512], P(None, 'chan'), may hold values from -0.375 to 0.375
- w_edge: bfloat16 [512, 512], P(None, 'chan'), may hold values from -0.25 to 0.25
- w_proc: bfloat16 [512, 512], P(None, 'chan'), may hold values from -0.25 to 0.25
- w_dec: bfloat16 [512, 512], P(None, 'chan'), may hold values from -0.25 to 0.25
- pack_rows: int32 [128, 4, 7, 384], P('patch', 'chan'), may hold values from 0 to 1023
- recv_node: int32 [128, 4, 7, 384], P('patch', 'chan'), may hold values from 0 to 512, as said below
- far_send: int32 [128, 4, 128, 8], P('patch', 'chan'), may hold values from 0 to 511
- far_recv: int32 [128, 4, 128, 8], P('patch', 'chan'), may hold values from 0 to 512, as said below
- loc_nbr: int32 [262144, 6], P(('patch', 'chan')), may hold values from 0 to 511
- dec_edge: int32 [524288, 3], P(('patch', 'chan')), may hold values from 0 to 3583
Outputs:
- grid_out: bfloat16 [524288, 512], P(('patch', 'chan'))
The draws below stay inside these ranges and needn't reach their ends.
Inputs may be any that keep to these rules, and one draw needn't show every extreme that they name: `recv_node`: within each [p, c, o] the live entries (under 512) come first and number at most 384; in every draw and for every c some patch p has 384 live entries at every o. `far_recv`: live entries (under 512) stand only where (p - q) or (q - p) modulo 128 is a positive power of two, and come first within each [p, c, q]; each such pair has 1 to 8 live entries, exactly 8 where (p - q) modulo 128 is 1.
All inputs are finite; a program needn't handle non-finite values.
Results may differ from the reference program's by a relative error of at most 0.0075.
Values may be sent and summed in bfloat16 or wider, within the bound.
No kernel may reach another device: no remote copies, remote signals or barrier semaphores. Data moves between devices by JAX's collectives and lax.ppermute only.
A program may use at most 64 MiB of HBM per device.

```python
import jax
import jax.numpy as jnp
from jax import lax

C_IN = 227
L = 512
G_DEV = 1024
M_DEV = 512
CAP = 384
FCAP = 8
KL = 6
KD = 3
NOFF = 7
GRID = 524288
MESH = 262144
N_PATCH = 128
N_CHAN = 4


def draw_recv_node(key, part):
    key = jax.random.fold_in(key, 11)
    key_one, key_two, key_three, key_four = jax.random.split(key, 4)
    halvings = jax.random.randint(key_one, (N_PATCH, N_CHAN), 0, 3)
    level = jnp.maximum(CAP // jnp.left_shift(jnp.ones_like(halvings), halvings), 1)
    busiest = jax.random.randint(key_two, (1, N_CHAN), 0, N_PATCH)
    patch_ids = jnp.arange(N_PATCH, dtype=jnp.int32)[:, None]
    is_busy = patch_ids == busiest
    level = jnp.where(is_busy, CAP, level)
    lowered = jax.random.randint(key_three, (N_PATCH, N_CHAN, NOFF), 0, 1 << 20) % (level[:, :, None] // 4 + 1)
    count = level[:, :, None] - jnp.where(is_busy[:, :, None], 0, lowered)
    slot_ids = jnp.arange(CAP, dtype=jnp.int32)[None, None, None, :]
    nodes = jax.random.randint(key_four, (N_PATCH, N_CHAN, NOFF, CAP), 0, M_DEV)
    return jnp.where(slot_ids < count[:, :, :, None], nodes, M_DEV).astype(jnp.int32)


def draw_far_recv(key, part):
    key = jax.random.fold_in(key, 23)
    key_one, key_two = jax.random.split(key, 2)
    receivers = jnp.arange(N_PATCH, dtype=jnp.int32)[:, None, None]
    senders = jnp.arange(N_PATCH, dtype=jnp.int32)[None, None, :]
    forward = (receivers - senders) % N_PATCH
    backward = (senders - receivers) % N_PATCH
    linked = (forward > 0) & (jnp.bitwise_and(forward, forward - 1) == 0) | (backward > 0) & (jnp.bitwise_and(backward, backward - 1) == 0)
    count = jax.random.randint(key_one, (N_PATCH, N_CHAN, N_PATCH), 1, FCAP + 1)
    count = jnp.where(forward == 1, FCAP, count)
    count = jnp.where(linked, count, 0)
    slot_ids = jnp.arange(FCAP, dtype=jnp.int32)[None, None, None, :]
    nodes = jax.random.randint(key_two, (N_PATCH, N_CHAN, N_PATCH, FCAP), 0, M_DEV)
    return jnp.where(slot_ids < count[:, :, :, None], nodes, M_DEV).astype(jnp.int32)


def touch_ends(values, stream_key, least, top_value):
    longest = values.shape.index(max(values.shape))
    spots = []
    for shift in (0, 1):
        where = [jax.random.randint(jax.random.fold_in(stream_key, axis), (), 0, length) for axis, length in enumerate(values.shape)]
        where[longest] = (where[longest] + shift) % values.shape[longest]
        spots.append(tuple(where))
    return values.at[spots[0]].set(least).at[spots[1]].set(top_value)


def shard_levels(stream_key, extent, shards, smallest, high):
    def one(position, shards_of):
        draws = jax.random.uniform(jax.random.fold_in(jax.random.fold_in(stream_key, 6), position), (shards_of,), jnp.float32, smallest / len(shards), high / len(shards))
        return jnp.repeat(jnp.exp(draws), extent[position] // shards_of).reshape((-1,) + (1,) * (len(extent) - position - 1))

    loudness = one(*shards[0])
    for cut in shards[1:]:
        loudness = loudness * one(*cut)
    return loudness


def bell_draw(rng, shape, scale, limit, shards=(), kind=jnp.bfloat16):
    factor_of = shard_levels(rng, shape, shards, -0.22, 0.18) if shards else 1.0
    array = jax.random.normal(rng, shape, jnp.float32) * scale * factor_of
    return jnp.minimum(jnp.maximum(array, -limit), limit).astype(kind)


def setup_inputs(seed: int = 0) -> dict:
    streams_of = jax.random.split(jax.random.key(seed), 13)
    return {
        "grid_in": bell_draw(streams_of[0], (GRID, C_IN), 1.0, 6.0, ((0, 512),)),
        "mesh_embed": bell_draw(streams_of[1], (MESH, L), 1.0, 6.0, ((0, 512),)),
        "w_embed": bell_draw(streams_of[2], (C_IN, L), C_IN ** -0.5, 0.375, ((1, 4),)),
        "w_edge": bell_draw(streams_of[3], (L, L), L ** -0.5, 0.25, ((1, 4),)),
        "w_proc": bell_draw(streams_of[4], (L, L), L ** -0.5, 0.25, ((1, 4),)),
        "w_dec": bell_draw(streams_of[5], (L, L), L ** -0.5, 0.25, ((1, 4),)),
        "pack_rows": touch_ends(jax.random.randint(streams_of[6], (N_PATCH, N_CHAN, NOFF, CAP), 0, G_DEV), jax.random.fold_in(streams_of[6], 1), 0, G_DEV - 1).astype(jnp.int32),
        "recv_node": draw_recv_node(jax.random.fold_in(streams_of[12], 71), 0),
        "far_send": touch_ends(jax.random.randint(streams_of[8], (N_PATCH, N_CHAN, N_PATCH, FCAP), 0, M_DEV), jax.random.fold_in(streams_of[8], 1), 0, M_DEV - 1).astype(jnp.int32),
        "far_recv": draw_far_recv(jax.random.fold_in(streams_of[12], 71), 0),
        "loc_nbr": touch_ends(jax.random.randint(streams_of[10], (MESH, KL), 0, M_DEV), jax.random.fold_in(streams_of[10], 1), 0, M_DEV - 1).astype(jnp.int32),
        "dec_edge": touch_ends(jax.random.randint(streams_of[11], (GRID, KD), 0, NOFF * M_DEV), jax.random.fold_in(streams_of[11], 1), 0, (NOFF * M_DEV) - 1).astype(jnp.int32),
    }


def one_group(grid_part, mesh_part, pack, recv, far_out, far_in, neighbours, dec_part, w_embed, w_edge, w_proc, w_dec):
    patches = grid_part.shape[0]
    grid_rows = grid_part.shape[1]
    mesh_rows = mesh_part.shape[1]
    offsets = pack.shape[1]
    reach = (offsets - 1) // 2
    channels = w_edge.shape[1]
    latent = jax.nn.silu(jnp.dot(grid_part.reshape(patches * grid_rows, -1), w_embed, preferred_element_type=jnp.float32)).astype(jnp.bfloat16)
    message = jax.nn.silu(jnp.dot(latent, w_edge, preferred_element_type=jnp.float32)).astype(jnp.bfloat16)
    patch_ids = jnp.arange(patches).astype(jnp.int32)
    offset_ids = jnp.arange(offsets).astype(jnp.int32)
    source = (patch_ids[:, None] - offset_ids[None, :] + reach) % patches
    chosen = pack[source, offset_ids[None, :]]
    sender_rows = (source[:, :, None] * grid_rows + chosen).reshape(-1)
    values = jnp.take(message, sender_rows, axis=0).astype(jnp.float32)
    target = jnp.where(recv < mesh_rows, patch_ids[:, None, None] * mesh_rows + recv, patches * mesh_rows).reshape(-1)
    summed = jax.ops.segment_sum(values, target, num_segments=patches * mesh_rows + 1)[:patches * mesh_rows]
    mesh_latent = (mesh_part.reshape(patches * mesh_rows, -1).astype(jnp.float32) + summed).astype(jnp.bfloat16)
    node_msg = jax.nn.silu(jnp.dot(mesh_latent, w_proc, preferred_element_type=jnp.float32)).astype(jnp.bfloat16)
    mesh_base = (patch_ids * mesh_rows)[:, None, None]
    local_rows = (mesh_base + neighbours).reshape(-1)
    local_sum = jnp.take(node_msg, local_rows, axis=0).astype(jnp.float32).reshape(patches * mesh_rows, -1, channels).sum(1)
    far_rows = jnp.swapaxes(mesh_base + far_out, 0, 1).reshape(-1)
    far_values = jnp.take(node_msg, far_rows, axis=0).astype(jnp.float32)
    far_target = jnp.where(far_in < mesh_rows, mesh_base + far_in, patches * mesh_rows).reshape(-1)
    far_sum = jax.ops.segment_sum(far_values, far_target, num_segments=patches * mesh_rows + 1)[:patches * mesh_rows]
    mesh_next = (mesh_latent.astype(jnp.float32) + local_sum + far_sum).astype(jnp.bfloat16)
    decoded = jax.nn.silu(jnp.dot(mesh_next, w_dec, preferred_element_type=jnp.float32)).astype(jnp.bfloat16)
    dec_flat = dec_part.reshape(patches * grid_rows, -1)
    which = dec_flat // mesh_rows
    node = dec_flat % mesh_rows
    row_patch = (jnp.arange(patches * grid_rows).astype(jnp.int32) // grid_rows)[:, None]
    source_patch = (row_patch + which - reach) % patches
    read_rows = (source_patch * mesh_rows + node).reshape(-1)
    grid_sum = jnp.take(decoded, read_rows, axis=0).astype(jnp.float32).reshape(patches * grid_rows, -1, channels).sum(1)
    return (latent.astype(jnp.float32) + grid_sum).astype(jnp.bfloat16)


def reference(grid_in, mesh_embed, w_embed, w_edge, w_proc, w_dec, pack_rows, recv_node, far_send, far_recv, loc_nbr, dec_edge):
    grid_blocks = jnp.moveaxis(grid_in.reshape(N_PATCH, N_CHAN, G_DEV, C_IN), 1, 0)
    mesh_blocks = jnp.moveaxis(mesh_embed.reshape(N_PATCH, N_CHAN, M_DEV, L), 1, 0)
    nbr_blocks = jnp.moveaxis(loc_nbr.reshape(N_PATCH, N_CHAN, M_DEV, KL), 1, 0)
    dec_blocks = jnp.moveaxis(dec_edge.reshape(N_PATCH, N_CHAN, G_DEV, KD), 1, 0)
    tables = (jnp.moveaxis(pack_rows, 1, 0), jnp.moveaxis(recv_node, 1, 0), jnp.moveaxis(far_send, 1, 0), jnp.moveaxis(far_recv, 1, 0))

    def run_group(pieces):
        grid_part, mesh_part, pack, recv, far_out, far_in, neighbours, dec_part = pieces
        return one_group(grid_part, mesh_part, pack, recv, far_out, far_in, neighbours, dec_part, w_embed, w_edge, w_proc, w_dec)

    result = lax.map(run_group, (grid_blocks, mesh_blocks) + tables + (nbr_blocks, dec_blocks))
    result = jnp.moveaxis(result.reshape(N_CHAN, N_PATCH, G_DEV, L), 0, 1)
    return result.reshape(N_PATCH * N_CHAN * G_DEV, L)
```

```python
import functools

import jax
import jax.numpy as jnp
from jax import lax
from jax.experimental import pallas as pl
from jax.experimental.pallas import tpu as pltpu
from jax.sharding import PartitionSpec as P

BF16 = jnp.bfloat16
F32 = jnp.float32
SENT = 240
WIDE = 256
FAR = (64, 32, -32, 16, -16, 8, -8, 4, -4, 2, -2, 1, -1)
VMEM = pltpu.CompilerParams(vmem_limit_bytes=56 * 1024 * 1024)


def silu(v):
    h = 0.5 * v
    return h + h * jnp.tanh(h)


def mul(a, b):
    return jnp.dot(a, b, preferred_element_type=F32)


def mul_nt(a, b):
    return lax.dot_general(a, b, (((1,), (1,)), ((), ())), preferred_element_type=F32)


def mul_tn(a, b):
    return lax.dot_general(a, b, (((0,), (0,)), ((), ())), preferred_element_type=F32)


def shifted(value, steps):
    count = lax.axis_size("patch")
    return lax.ppermute(value, "patch", [(i, (i + steps) % count) for i in range(count)])


def by_core(value, even_steps, odd_steps):
    count = lax.axis_size("patch")
    pairs = [(i, (i + (even_steps if i % 2 == 0 else odd_steps)) % count) for i in range(count)]
    return lax.ppermute(value, "patch", pairs)


def pack_body(core, x, pack, up, down, three, own, local, padded):
    here = core[0]
    channels, rows = x.shape
    slots = pack.shape[-1]
    padded[...] = jnp.zeros_like(padded)
    padded[0:channels, :] = x[...]
    row_of = lax.broadcasted_iota(jnp.int32, (rows, slots), 0)

    def chosen(offset):
        hot = jnp.where(row_of == pack[offset], 1.0, 0.0).astype(BF16)
        return mul(padded[...], hot).astype(BF16)

    up[0] = chosen(5)
    up[1] = chosen(jnp.where(here == 0, 6, 4))
    down[0] = chosen(1)
    down[1] = chosen(jnp.where(here == 0, 2, 0))
    three[...] = chosen(jnp.where(here == 0, 0, 6))
    own[...] = chosen(jnp.where(here == 0, 4, 2))
    local[...] = chosen(3)


def weights_body(embed, edge, proc, dec, out, padded):
    rows = embed.shape[0]
    padded[...] = jnp.zeros_like(padded)
    padded[0:rows, :] = embed[...]
    width = out.shape[0]
    eye = (
        lax.broadcasted_iota(jnp.int32, (width, width), 0)
        == lax.broadcasted_iota(jnp.int32, (width, width), 1)
    ).astype(F32).astype(BF16)
    at = 0
    for piece in (padded, edge, proc, dec):
        k = piece.shape[0]
        out[:, at : at + k] = mul_nt(eye, piece[...]).astype(BF16)
        at += k


def prepare_body(x, weights, edges, latent, table, padded):
    channels, rows = x.shape
    padded[...] = jnp.zeros_like(padded)
    padded[0:channels, :] = x[...]
    latent[...] = silu(
        lax.dot_general(
            padded[...], weights[:, 0:WIDE], (((0,), (1,)), ((), ())), preferred_element_type=F32
        )
    ).astype(BF16)
    count = edges.shape[0]
    columns = table.shape[1]
    spare = jnp.zeros((8 - count, rows), jnp.int32)
    ids = jnp.concatenate([edges[...], spare], axis=0).T
    step = 128
    for first in range(0, rows, step):
        for block in range(0, columns, 512):
            where = lax.broadcasted_iota(jnp.int32, (step, 512), 1) + block
            total = jnp.zeros((step, 512), F32)
            for k in range(count):
                total += jnp.where(where == ids[first : first + step, k : k + 1], 1.0, 0.0)
            table[first : first + step, block : block + 512] = total.astype(BF16)


def encode_body(
    core, here, local, up, down, three, sib, weights, recv, embed, far_ids, latent, message, far
):
    is_even = core[0] == 0
    nodes = embed.shape[0]
    slots = recv.shape[-1]
    w_embed = weights[:, 0:SENT]
    channels = weights.shape[0]
    w_edge = weights[:, WIDE : WIDE + channels]
    w_proc = weights[:, WIDE + channels : WIDE + 2 * channels]
    node_of = lax.broadcasted_iota(jnp.int32, (nodes, slots), 0)

    def summed(block, offset):
        rows = silu(mul(w_embed, block)).astype(BF16)
        sent = silu(mul(w_edge, rows)).astype(BF16)
        hot = jnp.where(node_of == recv[offset], 1.0, 0.0).astype(BF16)
        return mul_nt(hot, sent)

    total = embed[...].astype(F32)
    total += summed(local[...], 3)
    total += summed(up[0], 5)
    total += summed(down[0], 1)
    total += summed(three[...], jnp.where(is_even, 6, 0))
    total += summed(sib[0], jnp.where(is_even, 2, 4))
    total += summed(sib[1], jnp.where(is_even, 4, 6))
    total += summed(sib[2], jnp.where(is_even, 0, 2))
    rounded = total.astype(BF16)
    latent[...] = rounded
    sent = silu(mul_nt(rounded, w_proc)).astype(BF16)
    message[...] = sent
    hot = far_table(far_ids, here[0], 1, nodes)
    far[...] = mul(hot, sent).astype(BF16)


def far_table(ids, here, sign, nodes):
    count = ids.shape[1]
    column = lax.broadcasted_iota(jnp.int32, ids.shape, 1)
    node = lax.broadcasted_iota(jnp.int32, (ids.shape[0], nodes), 1)
    pieces = []
    for offset in FAR:
        partner = lax.rem(here + sign * offset + count, count)
        chosen = jnp.sum(jnp.where(column == partner, ids[...], 0), axis=1, keepdims=True)
        pieces.append(jnp.where(node == chosen, 1.0, 0.0))
    pieces.append(jnp.zeros_like(pieces[0]))
    return jnp.concatenate(pieces, axis=0).astype(BF16)


def local_body(latent, message, neighbours, out):
    nodes = latent.shape[0]
    count = neighbours.shape[0]
    spare = jnp.zeros((8 - count, nodes), jnp.int32)
    ids = jnp.concatenate([neighbours[...], spare], axis=0).T
    node = lax.broadcasted_iota(jnp.int32, (nodes, nodes), 1)
    table = jnp.zeros((nodes, nodes), F32)
    for k in range(count):
        table += jnp.where(node == ids[:, k : k + 1], 1.0, 0.0)
    out[...] = latent[...].astype(F32) + mul(table.astype(BF16), message[...])


def decode_body(here, base, far_ids, *rest):
    arrived, (weights, out) = rest[:-2], rest[-2:]
    nodes, channels = base.shape
    w_dec = weights[:, WIDE + 2 * channels :]
    hot = far_table(far_ids, here[0], -1, nodes)
    rows = [piece[...].astype(F32) for piece in arrived]
    rows.append(jnp.zeros_like(rows[0]))
    values = jnp.concatenate(rows, axis=0).astype(BF16)
    after = (base[...] + mul_tn(hot, values)).astype(BF16)
    out[...] = silu(mul_nt(after, w_dec)).astype(BF16)


def gather_body(core, latent, table, local, up, down, three, sib, out):
    is_even = core[0] == 0
    nodes = local.shape[0]

    def part(block, offset):
        at = pl.multiple_of(offset * nodes, nodes)
        return mul(table[:, pl.ds(at, nodes)], block)

    total = latent[...].astype(F32)
    total += part(local[...], 3)
    total += part(up[...], 1)
    total += part(down[...], 5)
    total += part(three[...], jnp.where(is_even, 0, 6))
    total += part(sib[0], jnp.where(is_even, 4, 2))
    total += part(sib[1], jnp.where(is_even, 2, 0))
    total += part(sib[2], jnp.where(is_even, 6, 4))
    out[...] = total.astype(BF16)


def call(body, out_shape, args, scratch=(), name=None):
    smem = pl.BlockSpec(memory_space=pltpu.SMEM)
    vmem = pl.BlockSpec(memory_space=pltpu.VMEM)
    specs = [smem if a.ndim == 1 else vmem for a in args]
    many = isinstance(out_shape, (list, tuple))
    return pl.pallas_call(
        body,
        out_shape=out_shape,
        in_specs=specs,
        out_specs=[vmem for _ in out_shape] if many else vmem,
        scratch_shapes=scratch,
        compiler_params=VMEM,
        name=name,
    )(*args)


def shape(*dims, kind=BF16):
    return jax.ShapeDtypeStruct(dims, kind)


def gather_weights(shard):
    patches, chans = lax.axis_size("patch"), lax.axis_size("chan")
    rows = shard.shape[0]
    half = rows // 2
    even = lax.axis_index("patch") % 2 == 0
    me = lax.axis_index("chan")

    def moved(value, even_steps, odd_steps):
        pairs = []
        for p in range(patches):
            steps = even_steps if p % 2 == 0 else odd_steps
            for c in range(chans):
                pairs.append((p * chans + c, p * chans + (c + steps) % chans))
        return lax.ppermute(value, ("patch", "chan"), pairs)

    near = moved(shard, 1, -1)
    part = moved(jnp.where(even, shard[:half], shard[half:]), 2, 2)
    both = by_core(jnp.concatenate([near, part], axis=0), 1, -1)
    near2, part2 = both[:rows], both[rows:]
    before = jnp.where(even, near, near2)
    after = jnp.where(even, near2, near)
    first = jnp.where(even, part, part2)
    second = jnp.where(even, part2, part)
    across = jnp.concatenate([first, second], axis=0)
    ring = jnp.stack([shard, after, across, before])
    order = (jnp.arange(chans) - me) % chans
    return jnp.take(ring, order, axis=0).reshape(chans * rows, -1)


def shards(
    grid_in,
    mesh_embed,
    w_embed,
    w_edge,
    w_proc,
    w_dec,
    pack_rows,
    recv_node,
    far_send,
    far_recv,
    loc_nbr,
    dec_edge,
):
    patch = lax.axis_index("patch").astype(jnp.int32)
    here = patch.reshape(1)
    core = (patch % 2).reshape(1)
    channels = mesh_embed.shape[1]
    nodes = mesh_embed.shape[0]
    rows = grid_in.shape[0]
    offsets, slots = pack_rows.shape[2:]
    x = grid_in.T
    pack = pack_rows.reshape(offsets, 1, slots)
    recv = recv_node.reshape(offsets, 1, slots)
    far_out_ids = far_send.reshape(far_send.shape[2:]).T
    far_in_ids = far_recv.reshape(far_recv.shape[2:]).T
    block = shape(SENT, slots)
    pair = shape(2, SENT, slots)

    shard = call(
        weights_body,
        shape(w_edge.shape[1], WIDE + 3 * channels),
        (w_embed, w_edge, w_proc, w_dec),
        [pltpu.VMEM((WIDE, w_edge.shape[1]), BF16)],
        name="weights",
    )
    up, down, three, own, local = call(
        pack_body,
        [pair, pair, block, block, block],
        (core, x, pack),
        [pltpu.VMEM((SENT, rows), BF16)],
        name="pack",
    )
    weights = lax.all_gather(shard, "chan", axis=0, tiled=True)
    up = shifted(up, 2)
    down = shifted(down, -2)
    three = by_core(three, -3, 3)
    sib = by_core(jnp.stack([own, up[1], down[1]]), 1, -1)
    latent, table = call(
        prepare_body,
        [shape(rows, channels), shape(rows, offsets * nodes)],
        (x, weights, dec_edge.T),
        [pltpu.VMEM((WIDE, rows), BF16)],
        name="prepare",
    )
    mesh_latent, node_msg, far_sent = call(
        encode_body,
        [shape(nodes, channels), shape(nodes, channels), shape(8 * len(FAR) + 8, channels)],
        (core, here, local, up, down, three, sib, weights, recv, mesh_embed, far_out_ids),
        name="encode",
    )
    arrived = [
        shifted(far_sent[8 * i : 8 * i + 8], offset) for i, offset in enumerate(FAR)
    ]
    base = call(
        local_body,
        shape(nodes, channels, kind=F32),
        (mesh_latent, node_msg, loc_nbr.T),
        name="short",
    )
    dec_msg = call(
        decode_body,
        shape(nodes, channels),
        (here, base, far_in_ids, *arrived, weights),
        name="decode",
    )
    up = shifted(dec_msg, 2)
    down = shifted(dec_msg, -2)
    three = by_core(dec_msg, -3, 3)
    sib = by_core(jnp.stack([dec_msg, up, down]), 1, -1)
    return call(
        gather_body,
        shape(rows, channels),
        (core, latent, table, dec_msg, up, down, three, sib),
        name="collect",
    )


def solution(mesh):
    both = P(("patch", "chan"), None)
    column = P(None, "chan")
    lists = P("patch", "chan", None, None)
    in_specs = (both, both, column, column, column, column, lists, lists, lists, lists, both, both)
    return jax.shard_map(shards, mesh=mesh, in_specs=in_specs, out_specs=both, check_vma=False)
```

```python
import functools

import jax
import jax.numpy as jnp
from jax import lax
from jax.experimental import pallas as pl
from jax.experimental.pallas import tpu as pltpu
from jax.sharding import PartitionSpec as P

BF16 = jnp.bfloat16
F32 = jnp.float32
SENT = 240
WIDE = 256
SPLIT = 128
FAR = ((16, 1, 2, None), (-16, -1, -2, None), (8, 4, 32, 64), (-8, -4, -32, None))
VMEM = pltpu.CompilerParams(vmem_limit_bytes=56 * 1024 * 1024)


def silu(v):
    h = 0.5 * v
    return h + h * jnp.tanh(h)


def mul(a, b):
    return jnp.dot(a, b, preferred_element_type=F32)


def mul_nt(a, b):
    return lax.dot_general(a, b, (((1,), (1,)), ((), ())), preferred_element_type=F32)


def mul_tn(a, b):
    return lax.dot_general(a, b, (((0,), (0,)), ((), ())), preferred_element_type=F32)


def shifted(value, steps):
    count = lax.axis_size("patch")
    return lax.ppermute(value, "patch", [(i, (i + steps) % count) for i in range(count)])


def by_core(value, even_steps, odd_steps):
    count = lax.axis_size("patch")
    pairs = [(i, (i + (even_steps if i % 2 == 0 else odd_steps)) % count) for i in range(count)]
    return lax.ppermute(value, "patch", pairs)


def silu_rows(weights, block):
    return silu(mul(weights, block)).astype(BF16)


def one_hot(where, ids):
    return jnp.where(where == ids, 1.0, 0.0).astype(BF16)


def pack_body(core, x, pack, up, down, three, own, padded):
    here = core[0]
    channels, rows = x.shape
    slots = pack.shape[-1]
    padded[...] = jnp.zeros_like(padded)
    padded[0:channels, :] = x[...]
    row_of = lax.broadcasted_iota(jnp.int32, (rows, slots), 0)

    def chosen(offset):
        return mul(padded[...], one_hot(row_of, pack[offset])).astype(BF16)

    up[0] = chosen(5)
    up[1] = chosen(jnp.where(here == 0, 6, 4))
    down[0] = chosen(1)
    down[1] = chosen(jnp.where(here == 0, 2, 0))
    three[...] = chosen(jnp.where(here == 0, 0, 6))
    own[...] = chosen(jnp.where(here == 0, 4, 2))


def weights_body(core, embed, edge, proc, dec, out, padded):
    width = out.shape[0]
    eye = one_hot(
        lax.broadcasted_iota(jnp.int32, (width, width), 0),
        lax.broadcasted_iota(jnp.int32, (width, width), 1),
    )

    def turn(piece, at):
        out[:, at : at + piece.shape[0]] = mul_nt(eye, piece).astype(BF16)

    @pl.when(core[0] == 0)
    def _():
        padded[...] = jnp.zeros_like(padded)
        padded[0 : embed.shape[0], :] = embed[...]
        turn(padded[...], 0)
        turn(edge[...], WIDE)
        turn(proc[0:SPLIT, :], WIDE + edge.shape[0])

    @pl.when(core[0] != 0)
    def _():
        turn(proc[SPLIT:, :], 0)
        turn(dec[...], proc.shape[0] - SPLIT)


def prepare_body(core, x, mine, other, edges, latent, table, padded):
    is_even = core[0] == 0
    channels, rows = x.shape
    padded[...] = jnp.zeros_like(padded)
    padded[0:channels, :] = x[...]
    w_embed = jnp.where(is_even, mine[:, 0:WIDE], other[:, 0:WIDE])
    latent[...] = silu(
        lax.dot_general(
            padded[...], w_embed, (((0,), (1,)), ((), ())), preferred_element_type=F32
        )
    ).astype(BF16)
    nodes = table.shape[1] // 3
    late = (jnp.where(is_even, 2, 0), jnp.where(is_even, 6, 4), jnp.where(is_even, 0, 6))
    for i, offset in enumerate(late):
        table[:, i * nodes : (i + 1) * nodes] = edge_table(edges, offset, nodes)


def edge_table(edges, offset, nodes):
    count, rows = edges.shape
    spare = jnp.zeros((8 - count, rows), jnp.int32)
    ids = jnp.concatenate([edges[...] - offset * nodes, spare], axis=0).T
    where = lax.broadcasted_iota(jnp.int32, (rows, nodes), 1)
    total = jnp.where(where == ids[:, 0:1], 1.0, 0.0)
    for k in range(1, count):
        total += jnp.where(where == ids[:, k : k + 1], 1.0, 0.0)
    return total.astype(BF16)


def messages(block, w_embed, w_edge):
    return silu_rows(w_edge, silu_rows(w_embed, block))


def early_body(core, x, pack, up, down, three, mine, other, recv, embed, out, padded):
    is_even = core[0] == 0
    nodes, channels = embed.shape
    slots = recv.shape[-1]
    w_embed = jnp.where(is_even, mine[:, 0:SENT], other[:, 0:SENT])
    w_edge = jnp.where(is_even, mine[:, WIDE : WIDE + channels], other[:, WIDE : WIDE + channels])
    padded[...] = jnp.zeros_like(padded)
    padded[0 : x.shape[0], :] = x[...]
    row_of = lax.broadcasted_iota(jnp.int32, (x.shape[1], slots), 0)
    local = mul(padded[...], one_hot(row_of, pack[3])).astype(BF16)
    node_of = lax.broadcasted_iota(jnp.int32, (nodes, slots), 0)
    total = embed[...].astype(F32)
    blocks = (
        (local, 3),
        (up[0], 5),
        (down[0], 1),
        (three[...], jnp.where(is_even, 6, 0)),
    )
    for block, offset in blocks:
        total += mul_nt(one_hot(node_of, recv[offset]), messages(block, w_embed, w_edge))
    out[...] = total


def encode_body(core, here, early, sib, mine, other, recv, far_ids, latent, message, far):
    is_even = core[0] == 0
    nodes, channels = early.shape
    slots = recv.shape[-1]
    w_embed = jnp.where(is_even, mine[:, 0:SENT], other[:, 0:SENT])
    w_edge = jnp.where(is_even, mine[:, WIDE : WIDE + channels], other[:, WIDE : WIDE + channels])
    first = WIDE + channels
    low = jnp.where(is_even, mine[:, first : first + SPLIT], other[:, first : first + SPLIT])
    rest = channels - SPLIT
    high = jnp.where(is_even, other[:, 0:rest], mine[:, 0:rest])
    w_proc = jnp.concatenate([low, high], axis=1)
    node_of = lax.broadcasted_iota(jnp.int32, (nodes, slots), 0)
    total = early[...]
    offsets = (jnp.where(is_even, 2, 4), jnp.where(is_even, 4, 6), jnp.where(is_even, 0, 2))
    for i, offset in enumerate(offsets):
        total += mul_nt(one_hot(node_of, recv[offset]), messages(sib[i], w_embed, w_edge))
    rounded = total.astype(BF16)
    latent[...] = rounded
    sent = silu(mul_nt(rounded, w_proc)).astype(BF16)
    message[...] = sent
    far[...] = mul(far_table(far_ids, here[0], 1, nodes), sent).astype(BF16)


def far_table(ids, here, sign, nodes):
    count = ids.shape[1]
    column = lax.broadcasted_iota(jnp.int32, ids.shape, 1)
    node = lax.broadcasted_iota(jnp.int32, (ids.shape[0], nodes), 1)
    pieces = []
    for offset in sum(FAR, ()):
        if offset is None:
            pieces.append(jnp.zeros((ids.shape[0], nodes), F32))
            continue
        partner = lax.rem(here + sign * offset + count, count)
        chosen = jnp.sum(jnp.where(column == partner, ids[...], 0), axis=1, keepdims=True)
        pieces.append(jnp.where(node == chosen, 1.0, 0.0))
    return jnp.concatenate(pieces, axis=0).astype(BF16)


def local_body(latent, message, neighbours, out):
    nodes = latent.shape[0]
    count = neighbours.shape[0]
    spare = jnp.zeros((8 - count, nodes), jnp.int32)
    ids = jnp.concatenate([neighbours[...], spare], axis=0).T
    node = lax.broadcasted_iota(jnp.int32, (nodes, nodes), 1)
    table = jnp.where(node == ids[:, 0:1], 1.0, 0.0)
    for k in range(1, count):
        table += jnp.where(node == ids[:, k : k + 1], 1.0, 0.0)
    out[...] = latent[...].astype(F32) + mul(table.astype(BF16), message[...])


def decode_body(core, here, base, far_ids, arrived, mine, other, out):
    nodes, channels = base.shape
    at = channels - SPLIT
    w_dec = jnp.where(core[0] == 0, other[:, at : at + channels], mine[:, at : at + channels])
    hot = far_table(far_ids, here[0], -1, nodes)
    after = (base[...] + mul_tn(hot, arrived[...])).astype(BF16)
    out[...] = silu(mul_nt(after, w_dec)).astype(BF16)


def near_body(core, latent, edges, local, sib, up, down, out):
    is_even = core[0] == 0
    nodes = local.shape[0]
    total = latent[...].astype(F32)
    blocks = ((local, 3), (sib, jnp.where(is_even, 4, 2)), (up, 1), (down, 5))
    for block, offset in blocks:
        total += mul(edge_table(edges, offset, nodes), block[...])
    out[...] = total


def collect_body(near, table, relay, three, out):
    nodes = three.shape[0]
    total = near[...]
    for i, block in enumerate((relay[0], relay[1], three[...])):
        total += mul(table[:, i * nodes : (i + 1) * nodes], block)
    out[...] = total.astype(BF16)


def call(body, out_shape, args, scratch=(), name=None):
    smem = pl.BlockSpec(memory_space=pltpu.SMEM)
    vmem = pl.BlockSpec(memory_space=pltpu.VMEM)
    specs = [smem if a.ndim == 1 else vmem for a in args]
    many = isinstance(out_shape, (list, tuple))
    return pl.pallas_call(
        body,
        out_shape=out_shape,
        in_specs=specs,
        out_specs=[vmem for _ in out_shape] if many else vmem,
        scratch_shapes=scratch,
        compiler_params=VMEM,
        name=name,
    )(*args)


def shape(*dims, kind=BF16):
    return jax.ShapeDtypeStruct(dims, kind)


def far_exchange(rows):
    patches, chans = lax.axis_size("patch"), lax.axis_size("chan")
    kinds = len(FAR[0])
    count, channels = rows.shape
    each = count // (chans * kinds)
    mine = lax.all_to_all(
        rows.reshape(chans, kinds * each, channels), "chan", 0, 0, tiled=True
    ).reshape(chans, kinds, each, channels)
    arrived = []
    for kind in range(kinds):
        pairs = []
        for c in range(chans):
            if FAR[c][kind] is None:
                continue
            for p in range(patches):
                pairs.append((p * chans + c, (p + FAR[c][kind]) % patches * chans + c))
        arrived.append(lax.ppermute(mine[:, kind], ("patch", "chan"), pairs))
    back = jnp.stack(arrived, axis=1).reshape(chans, kinds * each, channels)
    return lax.all_to_all(back, "chan", 0, 0, tiled=True).reshape(count, channels)


def shards(
    grid_in,
    mesh_embed,
    w_embed,
    w_edge,
    w_proc,
    w_dec,
    pack_rows,
    recv_node,
    far_send,
    far_recv,
    loc_nbr,
    dec_edge,
):
    patch = lax.axis_index("patch").astype(jnp.int32)
    here = patch.reshape(1)
    core = (patch % 2).reshape(1)
    channels = mesh_embed.shape[1]
    nodes = mesh_embed.shape[0]
    rows = grid_in.shape[0]
    offsets, slots = pack_rows.shape[2:]
    x = grid_in.T
    pack = pack_rows.reshape(offsets, 1, slots)
    recv = recv_node.reshape(offsets, 1, slots)
    far_out_ids = far_send.reshape(far_send.shape[2:]).T
    far_in_ids = far_recv.reshape(far_recv.shape[2:]).T
    block = shape(SENT, slots)
    pair = shape(2, SENT, slots)
    padded = pltpu.VMEM((SENT, rows), BF16)

    up, down, three, own = call(
        pack_body, [pair, pair, block, block], (core, x, pack), [padded], name="pack"
    )
    up, down, three, own, w_embed, w_edge, w_proc, w_dec = lax.optimization_barrier(
        (up, down, three, own, w_embed, w_edge, w_proc, w_dec)
    )
    three = by_core(three, -3, 3)
    up = shifted(up, 2)
    down = shifted(down, -2)
    shard = call(
        weights_body,
        shape(w_edge.shape[1], (WIDE + 3 * channels) // 2),
        (core, w_embed, w_edge, w_proc, w_dec),
        [pltpu.VMEM((WIDE, w_edge.shape[1]), BF16)],
        name="weights",
    )
    mine = lax.all_gather(shard, "chan", axis=0, tiled=True)
    mine, up, down, three = lax.optimization_barrier((mine, up, down, three))
    sib = by_core(jnp.stack([own, up[1], down[1]]), 1, -1)
    other = by_core(mine, 1, -1)
    early = call(
        early_body,
        shape(nodes, channels, kind=F32),
        (core, x, pack, up, down, three, mine, other, recv, mesh_embed),
        [padded],
        name="early",
    )
    mesh_latent, node_msg, far_sent = call(
        encode_body,
        [shape(nodes, channels), shape(nodes, channels), shape(8 * 16, channels)],
        (core, here, early, sib, mine, other, recv, far_out_ids),
        name="encode",
    )
    arrived = far_exchange(far_sent)
    base = call(
        local_body,
        shape(nodes, channels, kind=F32),
        (mesh_latent, node_msg, loc_nbr.T),
        name="short",
    )
    dec_msg = call(
        decode_body,
        shape(nodes, channels),
        (core, here, base, far_in_ids, arrived, mine, other),
        name="decode",
    )
    up = shifted(dec_msg, 2)
    down = shifted(dec_msg, -2)
    sib = by_core(dec_msg, 1, -1)
    latent, table = call(
        prepare_body,
        [shape(rows, channels), shape(rows, 3 * nodes)],
        (core, x, mine, other, dec_edge.T),
        [pltpu.VMEM((WIDE, rows), BF16)],
        name="prepare",
    )
    up, down, sib, latent, table = lax.optimization_barrier((up, down, sib, latent, table))
    three = by_core(jnp.where(core[0] == 0, down, up), -1, 1)
    relay = by_core(jnp.stack([up, down]), 1, -1)
    near = call(
        near_body,
        shape(rows, channels, kind=F32),
        (core, latent, dec_edge.T, dec_msg, sib, up, down),
        name="near",
    )
    return call(
        collect_body,
        shape(rows, channels),
        (near, table, relay, three),
        name="collect",
    )


def solution(mesh):
    both = P(("patch", "chan"), None)
    column = P(None, "chan")
    lists = P("patch", "chan", None, None)
    in_specs = (both, both, column, column, column, column, lists, lists, lists, lists, both, both)
    return jax.shard_map(shards, mesh=mesh, in_specs=in_specs, out_specs=both, check_vma=False)
```

```python
import functools

import jax
import jax.numpy as jnp
from jax import lax
from jax.experimental import pallas as pl
from jax.experimental.pallas import tpu as pltpu
from jax.sharding import PartitionSpec as P

BF16 = jnp.bfloat16
F32 = jnp.float32
SENT = 240
WIDE = 256
SPLIT = 128
FAR = ((16, 1, 2, None), (-16, -1, -2, None), (8, 4, 32, 64), (-8, -4, -32, None))
VMEM = pltpu.CompilerParams(vmem_limit_bytes=20 * 1024 * 1024)


def silu(v):
    h = 0.5 * v
    return h + h * jnp.tanh(h)


def mul(a, b):
    return jnp.dot(a, b, preferred_element_type=F32)


def mul_nt(a, b):
    return lax.dot_general(a, b, (((1,), (1,)), ((), ())), preferred_element_type=F32)


def mul_tn(a, b):
    return lax.dot_general(a, b, (((0,), (0,)), ((), ())), preferred_element_type=F32)


def shifted(value, steps):
    count = lax.axis_size("patch")
    return lax.ppermute(value, "patch", [(i, (i + steps) % count) for i in range(count)])


def by_core(value, even_steps, odd_steps):
    count = lax.axis_size("patch")
    pairs = [(i, (i + (even_steps if i % 2 == 0 else odd_steps)) % count) for i in range(count)]
    return lax.ppermute(value, "patch", pairs)


def silu_rows(weights, block):
    return silu(mul(weights, block)).astype(BF16)


def one_hot(where, ids):
    same = where == jnp.broadcast_to(ids.astype(jnp.int16), where.shape)
    return jnp.where(same, jnp.ones(where.shape, BF16), jnp.zeros(where.shape, BF16))


def positions(dims, axis):
    return lax.broadcasted_iota(jnp.int32, dims, axis).astype(jnp.int16)


def pack_body(core, x, pack, up, down, three, own, hot):
    here = core[0]
    channels, rows = x.shape
    slots = pack.shape[-1]
    row_of = positions((rows, slots), 0)
    blank = jnp.zeros((SENT - channels, slots), BF16)

    def chosen(outs, offsets):
        for i, offset in enumerate(offsets):
            hot[:, i * slots : (i + 1) * slots] = one_hot(row_of, pack[offset])
        found = mul(x[...], hot[...]).astype(BF16)
        for i, out in enumerate(outs):
            out[0:channels, :] = found[:, i * slots : (i + 1) * slots]
            out[channels:SENT, :] = blank

    chosen((up.at[0], up.at[1]), (5, jnp.where(here == 0, 6, 4)))
    chosen((down.at[0], down.at[1]), (1, jnp.where(here == 0, 2, 0)))
    chosen((three, own), (jnp.where(here == 0, 0, 6), jnp.where(here == 0, 4, 2)))


def weights_body(core, embed, edge, proc, dec, out, padded):
    width = out.shape[0]
    eye = one_hot(
        positions((width, width), 0), lax.broadcasted_iota(jnp.int32, (width, width), 1)
    )

    def turn(piece, at):
        out[:, at : at + piece.shape[0]] = mul_nt(eye, piece).astype(BF16)

    @pl.when(core[0] == 0)
    def _():
        padded[...] = jnp.zeros_like(padded)
        padded[0 : embed.shape[0], :] = embed[...]
        turn(padded[...], 0)
        turn(edge[...], WIDE)
        turn(proc[0:SPLIT, :], WIDE + edge.shape[0])

    @pl.when(core[0] != 0)
    def _():
        turn(proc[SPLIT:, :], 0)
        turn(dec[...], proc.shape[0] - SPLIT)


def prepare_body(core, mine, other, x, edges, latent, *rest):
    *tables, padded = rest
    is_even = core[0] == 0
    channels, rows = x.shape
    padded[...] = jnp.zeros_like(padded)
    padded[0:channels, :] = x[...]
    w_embed = jnp.where(is_even, mine[:, 0:WIDE], other[:, 0:WIDE])
    latent[...] = silu(
        lax.dot_general(
            padded[...], w_embed, (((0,), (1,)), ((), ())), preferred_element_type=F32
        )
    ).astype(BF16)
    order = (
        3,
        jnp.where(is_even, 4, 2),
        1,
        5,
        jnp.where(is_even, 0, 6),
        jnp.where(is_even, 2, 0),
        jnp.where(is_even, 6, 4),
    )
    count = edges.shape[0]
    spare = jnp.zeros((8 - count, rows), jnp.int32)
    ids = jnp.concatenate([edges[...], spare], axis=0).T
    nodes = sum(table.shape[1] for table in tables) // len(order)
    step = 128
    columns = positions((step, step), 1)
    for first in range(0, rows, step):
        wide = [
            jnp.broadcast_to(ids[first : first + step, k : k + 1], (step, step))
            for k in range(count)
        ]
        at = 0
        for table in tables:
            for block in range(table.shape[1] // nodes):
                base = order[at] * nodes
                moved = [(w - base).astype(jnp.int16) for w in wide]
                at += 1
                for part in range(0, nodes, step):
                    here = columns + jnp.int16(part)
                    total = one_hot(here, moved[0])
                    for k in range(1, count):
                        total += one_hot(here, moved[k])
                    left = block * nodes + part
                    table[first : first + step, left : left + step] = total


def messages(blocks, w_embed, w_edge, rows, sent):
    slots = blocks[0].shape[1]
    for i, block in enumerate(blocks):
        rows[:, i * slots : (i + 1) * slots] = silu_rows(w_embed, block)
    for i in range(len(blocks)):
        at = slice(i * slots, (i + 1) * slots)
        sent[:, at] = silu_rows(w_edge, rows[:, at])


def receivers(recv, offsets, hot):
    nodes, slots = hot.shape[0], recv.shape[-1]
    node_of = positions((nodes, slots), 0)
    for i, offset in enumerate(offsets):
        hot[:, i * slots : (i + 1) * slots] = one_hot(node_of, recv[offset])


def early_body(
    core, x, pack, up, down, three, mine, other, recv, embed, out, rows, sent, hot, padded
):
    is_even = core[0] == 0
    nodes, channels = embed.shape
    slots = recv.shape[-1]
    w_embed = jnp.where(is_even, mine[:, 0:SENT], other[:, 0:SENT])
    w_edge = jnp.where(is_even, mine[:, WIDE : WIDE + channels], other[:, WIDE : WIDE + channels])
    padded[...] = jnp.zeros_like(padded)
    padded[0 : x.shape[0], :] = x[...]
    local = mul(padded[...], one_hot(positions((x.shape[1], slots), 0), pack[3])).astype(BF16)
    messages((local, up[0], down[0], three[...]), w_embed, w_edge, rows, sent)
    receivers(recv, (3, 5, 1, jnp.where(is_even, 6, 0)), hot)
    out[...] = embed[...].astype(F32) + mul_nt(hot[...], sent[...])


def encode_body(
    core, here, early, sib, mine, other, recv, far_ids, latent, message, far, rows, sent, hot
):
    is_even = core[0] == 0
    nodes, channels = early.shape
    w_embed = jnp.where(is_even, mine[:, 0:SENT], other[:, 0:SENT])
    w_edge = jnp.where(is_even, mine[:, WIDE : WIDE + channels], other[:, WIDE : WIDE + channels])
    first = WIDE + channels
    low = jnp.where(is_even, mine[:, first : first + SPLIT], other[:, first : first + SPLIT])
    rest = channels - SPLIT
    high = jnp.where(is_even, other[:, 0:rest], mine[:, 0:rest])
    w_proc = jnp.concatenate([low, high], axis=1)
    messages((sib[0], sib[1], sib[2]), w_embed, w_edge, rows, sent)
    offsets = (jnp.where(is_even, 2, 4), jnp.where(is_even, 4, 6), jnp.where(is_even, 0, 2))
    receivers(recv, offsets, hot)
    rounded = (early[...] + mul_nt(hot[...], sent[...])).astype(BF16)
    latent[...] = rounded
    made = silu(mul_nt(rounded, w_proc)).astype(BF16)
    message[...] = made
    far[...] = mul(far_table(far_ids, here[0], 1, nodes), made).astype(BF16)


def far_table(ids, here, sign, nodes):
    count = ids.shape[1]
    column = lax.broadcasted_iota(jnp.int32, ids.shape, 1)
    node = lax.broadcasted_iota(jnp.int32, (ids.shape[0], nodes), 1)
    pieces = []
    for offset in sum(FAR, ()):
        if offset is None:
            pieces.append(jnp.zeros((ids.shape[0], nodes), F32))
            continue
        partner = lax.rem(here + sign * offset + count, count)
        chosen = jnp.sum(jnp.where(column == partner, ids[...], 0), axis=1, keepdims=True)
        pieces.append(jnp.where(node == chosen, 1.0, 0.0))
    return jnp.concatenate(pieces, axis=0).astype(BF16)


def local_body(latent, message, neighbours, out):
    nodes = latent.shape[0]
    count = neighbours.shape[0]
    spare = jnp.zeros((8 - count, nodes), jnp.int32)
    ids = jnp.concatenate([neighbours[...], spare], axis=0).T
    node = lax.broadcasted_iota(jnp.int32, (nodes, nodes), 1)
    table = jnp.where(node == ids[:, 0:1], 1.0, 0.0)
    for k in range(1, count):
        table += jnp.where(node == ids[:, k : k + 1], 1.0, 0.0)
    out[...] = latent[...].astype(F32) + mul(table.astype(BF16), message[...])


def decode_body(core, here, base, far_ids, arrived, mine, other, out):
    nodes, channels = base.shape
    at = channels - SPLIT
    w_dec = jnp.where(core[0] == 0, other[:, at : at + channels], mine[:, at : at + channels])
    hot = far_table(far_ids, here[0], -1, nodes)
    after = (base[...] + mul_tn(hot, arrived[...])).astype(BF16)
    out[...] = silu(mul_nt(after, w_dec)).astype(BF16)


def add_body(before, *rest):
    *blocks, table, out, joined = rest
    nodes = blocks[0].shape[0]
    for i, block in enumerate(blocks):
        joined[i * nodes : (i + 1) * nodes, :] = block[...]
    out[...] = (before[...].astype(F32) + mul(table[...], joined[...])).astype(out.dtype)


def call(body, out_shape, args, scratch=(), name=None, stored=()):
    near = len(args)
    args = (*args, *stored)
    smem = pl.BlockSpec(memory_space=pltpu.SMEM)
    vmem = pl.BlockSpec(memory_space=pltpu.VMEM)
    many = isinstance(out_shape, (list, tuple))
    args = [
        a if a.ndim == 1 else pltpu.with_memory_space_constraint(a, place)
        for a, place in zip(args, [pltpu.VMEM] * near + [pltpu.HBM] * (len(args) - near))
    ]
    return pl.pallas_call(
        body,
        out_shape=out_shape,
        in_specs=[smem if a.ndim == 1 else vmem for a in args],
        out_specs=[vmem for _ in out_shape] if many else vmem,
        scratch_shapes=scratch,
        compiler_params=VMEM,
        name=name,
    )(*args)


def shape(*dims, kind=BF16):
    return pltpu.VMEM(dims, kind)


def far_exchange(rows):
    patches, chans = lax.axis_size("patch"), lax.axis_size("chan")
    kinds = len(FAR[0])
    count, channels = rows.shape
    each = count // (chans * kinds)
    mine = lax.all_to_all(
        rows.reshape(chans, kinds * each, channels), "chan", 0, 0, tiled=True
    ).reshape(chans, kinds, each, channels)
    arrived = []
    for kind in range(kinds):
        pairs = []
        for c in range(chans):
            if FAR[c][kind] is None:
                continue
            for p in range(patches):
                pairs.append((p * chans + c, (p + FAR[c][kind]) % patches * chans + c))
        arrived.append(lax.ppermute(mine[:, kind], ("patch", "chan"), pairs))
    back = jnp.stack(arrived, axis=1).reshape(chans, kinds * each, channels)
    return lax.all_to_all(back, "chan", 0, 0, tiled=True).reshape(count, channels)


def shards(
    grid_in,
    mesh_embed,
    w_embed,
    w_edge,
    w_proc,
    w_dec,
    pack_rows,
    recv_node,
    far_send,
    far_recv,
    loc_nbr,
    dec_edge,
):
    patch = lax.axis_index("patch").astype(jnp.int32)
    here = patch.reshape(1)
    core = (patch % 2).reshape(1)
    channels = mesh_embed.shape[1]
    nodes = mesh_embed.shape[0]
    rows = grid_in.shape[0]
    offsets, slots = pack_rows.shape[2:]
    x = grid_in.T
    pack = pack_rows.reshape(offsets, 1, slots)
    recv = recv_node.reshape(offsets, 1, slots)
    far_out_ids = far_send.reshape(far_send.shape[2:]).T
    far_in_ids = far_recv.reshape(far_recv.shape[2:]).T
    def stored(*dims):
        return pltpu.HBM(dims, BF16)

    def work(blocks):
        wide = pltpu.VMEM((channels, blocks * slots), BF16)
        return wide, wide, pltpu.VMEM((nodes, blocks * slots), BF16)

    block = shape(SENT, slots)
    pair = shape(2, SENT, slots)
    padded = pltpu.VMEM((SENT, rows), BF16)

    up, down, three, own = call(
        pack_body,
        [pair, pair, block, block],
        (core,),
        [pltpu.VMEM((rows, 2 * slots), BF16)],
        name="pack",
        stored=(x, pack),
    )
    up, down, three, own, w_embed, w_edge, w_proc, w_dec = lax.optimization_barrier(
        (up, down, three, own, w_embed, w_edge, w_proc, w_dec)
    )
    three = by_core(three, -3, 3)
    up = shifted(up, 2)
    down = shifted(down, -2)
    shard = call(
        weights_body,
        shape(w_edge.shape[1], (WIDE + 3 * channels) // 2),
        (core,),
        [pltpu.VMEM((WIDE, w_edge.shape[1]), BF16)],
        name="weights",
        stored=(w_embed, w_edge, w_proc, w_dec),
    )
    mine = lax.all_gather(shard, "chan", axis=0, tiled=True)
    mine, up, down, three = lax.optimization_barrier((mine, up, down, three))
    sib = by_core(jnp.stack([own, up[1], down[1]]), 1, -1)
    other = by_core(mine, 1, -1)
    early = call(
        early_body,
        shape(nodes, channels, kind=F32),
        (core, x, pack, up, down, three, mine, other, recv, mesh_embed),
        [*work(4), padded],
        name="early",
    )
    mesh_latent, node_msg, far_sent = call(
        encode_body,
        [stored(nodes, channels), stored(nodes, channels), shape(8 * 16, channels)],
        (core, here, early, sib, mine, other, recv, far_out_ids),
        [*work(3)],
        name="encode",
    )
    arrived = far_exchange(far_sent)
    base = call(
        local_body,
        shape(nodes, channels, kind=F32),
        (),
        name="short",
        stored=(mesh_latent, node_msg, loc_nbr.T),
    )
    dec_msg = call(
        decode_body,
        shape(nodes, channels),
        (core, here, base, far_in_ids, arrived, mine, other),
        name="decode",
    )
    up = shifted(dec_msg, 2)
    down = shifted(dec_msg, -2)
    sib = by_core(dec_msg, 1, -1)
    dec_msg, x, edges = lax.optimization_barrier((dec_msg, x, dec_edge.T))
    latent, own_table, near_table, late_table = call(
        prepare_body,
        [shape(rows, channels)] + [shape(rows, n * nodes) for n in (2, 2, 3)],
        (core, mine, other),
        [pltpu.VMEM((WIDE, rows), BF16)],
        name="prepare",
        stored=(x, edges),
    )

    def added(name, before, blocks, table, kind=F32):
        return call(
            add_body,
            shape(rows, channels, kind=kind) if kind == F32 else stored(rows, channels),
            (before, *blocks, table),
            [pltpu.VMEM((len(blocks) * nodes, channels), BF16)],
            name=name,
        )

    total = added("own", latent, (dec_msg, sib), own_table)
    up, down, total = lax.optimization_barrier((up, down, total))
    three = by_core(jnp.where(core[0] == 0, down, up), -1, 1)
    relay_up = by_core(up, 1, -1)
    relay_down = by_core(down, 1, -1)
    total = added("near", total, (up, down), near_table)
    return added("collect", total, (three, relay_up, relay_down), late_table, BF16)


def solution(mesh):
    both = P(("patch", "chan"), None)
    column = P(None, "chan")
    lists = P("patch", "chan", None, None)
    in_specs = (both, both, column, column, column, column, lists, lists, lists, lists, both, both)
    return jax.shard_map(shards, mesh=mesh, in_specs=in_specs, out_specs=both, check_vma=False)
```

```python
import functools

import jax
import jax.numpy as jnp
from jax import lax
from jax.experimental import pallas as pl
from jax.experimental.pallas import tpu as pltpu
from jax.sharding import PartitionSpec as P

BF16 = jnp.bfloat16
F32 = jnp.float32
SENT = 240
WIDE = 256
FAR = ((None, 2, 1, 16), (None, -2, -1, -16), (64, 32, 4, 8), (None, -32, -4, -8))
VMEM = pltpu.CompilerParams(vmem_limit_bytes=20 * 1024 * 1024)


def silu(v):
    h = 0.5 * v
    return h + h * jnp.tanh(h)


def mul(a, b):
    return jnp.dot(a, b, preferred_element_type=F32)


def mul_nt(a, b):
    return lax.dot_general(a, b, (((1,), (1,)), ((), ())), preferred_element_type=F32)


def mul_tn(a, b):
    return lax.dot_general(a, b, (((0,), (0,)), ((), ())), preferred_element_type=F32)


def shifted(value, steps):
    count = lax.axis_size("patch")
    return lax.ppermute(value, "patch", [(i, (i + steps) % count) for i in range(count)])


def by_core(value, even_steps, odd_steps):
    count = lax.axis_size("patch")
    pairs = [(i, (i + (even_steps if i % 2 == 0 else odd_steps)) % count) for i in range(count)]
    return lax.ppermute(value, "patch", pairs)


def silu_rows(weights, block):
    return silu(mul(weights, block)).astype(BF16)


def one_hot(where, ids):
    same = where == jnp.broadcast_to(ids.astype(jnp.int16), where.shape)
    return jnp.where(same, jnp.ones(where.shape, BF16), jnp.zeros(where.shape, BF16))


def positions(dims, axis):
    return lax.broadcasted_iota(jnp.int32, dims, axis).astype(jnp.int16)


def pack_body(core, x, pack, three, up, down, own, hot):
    here = core[0]
    channels, rows = x.shape
    slots = pack.shape[-1]
    row_of = positions((rows, slots), 0)
    blank = jnp.zeros((SENT - channels, slots), BF16)

    def chosen(outs, offsets):
        for i, offset in enumerate(offsets):
            hot[:, i * slots : (i + 1) * slots] = one_hot(row_of, pack[offset])
        found = mul(x[...], hot[...]).astype(BF16)
        for i, out in enumerate(outs):
            out[0:channels, :] = found[:, i * slots : (i + 1) * slots]
            out[channels:SENT, :] = blank

    chosen((up.at[0], up.at[1]), (5, jnp.where(here == 0, 6, 4)))
    chosen((down.at[0], down.at[1]), (1, jnp.where(here == 0, 2, 0)))
    chosen((three, own), (jnp.where(here == 0, 0, 6), jnp.where(here == 0, 4, 2)))


def weights_body(embed, edge, proc, dec, out, padded):
    copies, width, columns = out.shape
    eye = one_hot(
        positions((width, width), 0), lax.broadcasted_iota(jnp.int32, (width, width), 1)
    )
    padded[...] = jnp.zeros_like(padded)
    padded[0 : embed.shape[0], :] = embed[...]
    at = 0
    for piece in (padded, edge, proc, dec):
        turned = mul_nt(eye, piece[...]).astype(BF16)
        for i in range(copies):
            out[i, :, at : at + piece.shape[0]] = turned
        at += piece.shape[0]


def tables_body(core, edges, *tables):
    is_even = core[0] == 0
    rows = edges.shape[1]
    order = (
        3,
        jnp.where(is_even, 4, 2),
        jnp.where(is_even, 5, 1),
        jnp.where(is_even, 1, 5),
        jnp.where(is_even, 0, 6),
        jnp.where(is_even, 2, 4),
        jnp.where(is_even, 6, 0),
    )
    count = edges.shape[0]
    spare = jnp.zeros((8 - count, rows), jnp.int32)
    ids = jnp.concatenate([edges[...], spare], axis=0).T
    nodes = sum(table.shape[1] for table in tables) // len(order)
    step = 128
    columns = positions((step, step), 1)
    for first in range(0, rows, step):
        wide = [
            jnp.broadcast_to(ids[first : first + step, k : k + 1], (step, step))
            for k in range(count)
        ]
        at = 0
        for table in tables:
            for block in range(table.shape[1] // nodes):
                base = order[at] * nodes
                moved = [(w - base).astype(jnp.int16) for w in wide]
                at += 1
                for part in range(0, nodes, step):
                    here = columns + jnp.int16(part)
                    total = one_hot(here, moved[0])
                    for k in range(1, count):
                        total += one_hot(here, moved[k])
                    left = block * nodes + part
                    table[first : first + step, left : left + step] = total


def messages(blocks, w_embed, w_edge, rows, sent):
    slots = blocks[0].shape[1]
    for i, block in enumerate(blocks):
        rows[:, i * slots : (i + 1) * slots] = silu_rows(w_embed, block)
    for i in range(len(blocks)):
        at = slice(i * slots, (i + 1) * slots)
        sent[:, at] = silu_rows(w_edge, rows[:, at])


def receivers(recv, offsets, hot):
    nodes, slots = hot.shape[0], recv.shape[-1]
    node_of = positions((nodes, slots), 0)
    for i, offset in enumerate(offsets):
        hot[:, i * slots : (i + 1) * slots] = one_hot(node_of, recv[offset])


def early_body(
    core, x, pack, up, down, three, weights, recv, embed, out, rows, sent, hot, padded, near, arrived
):
    is_even = core[0] == 0
    nodes, channels = embed.shape
    fetch = pltpu.make_async_copy(embed, near, arrived)
    fetch.start()
    slots = recv.shape[-1]
    w_embed = weights[:, 0:SENT]
    w_edge = weights[:, WIDE : WIDE + channels]
    padded[...] = jnp.zeros_like(padded)
    padded[0 : x.shape[0], :] = x[...]
    local = mul(padded[...], one_hot(positions((x.shape[1], slots), 0), pack[3])).astype(BF16)
    messages((local, up[0], down[0], three[...]), w_embed, w_edge, rows, sent)
    receivers(recv, (3, 5, 1, jnp.where(is_even, 6, 0)), hot)
    total = mul_nt(hot[...], sent[...])
    fetch.wait()
    out[...] = near[...].astype(F32) + total


def encode_body(
    core, here, early, sib, weights, recv, far_ids, latent, message, far, rows, sent, hot
):
    is_even = core[0] == 0
    nodes, channels = early.shape
    w_embed = weights[:, 0:SENT]
    w_edge = weights[:, WIDE : WIDE + channels]
    messages((sib[0], sib[1], sib[2]), w_embed, w_edge, rows, sent)
    offsets = (jnp.where(is_even, 2, 4), jnp.where(is_even, 4, 6), jnp.where(is_even, 0, 2))
    receivers(recv, offsets, hot)
    rounded = (early[...] + mul_nt(hot[...], sent[...])).astype(BF16)
    latent[...] = rounded
    w_proc = weights[:, WIDE + channels : WIDE + 2 * channels]
    made = silu(mul_nt(rounded, w_proc)).astype(BF16)
    message[...] = made
    far[...] = mul(far_table(far_ids, here[0], 1, nodes), made).astype(BF16)


def far_table(ids, here, sign, nodes):
    count = ids.shape[1]
    column = lax.broadcasted_iota(jnp.int32, ids.shape, 1)
    node = lax.broadcasted_iota(jnp.int32, (ids.shape[0], nodes), 1)
    pieces = []
    for offset in sum(FAR, ()):
        if offset is None:
            pieces.append(jnp.zeros((ids.shape[0], nodes), F32))
            continue
        partner = lax.rem(here + sign * offset + count, count)
        chosen = jnp.sum(jnp.where(column == partner, ids[...], 0), axis=1, keepdims=True)
        pieces.append(jnp.where(node == chosen, 1.0, 0.0))
    return jnp.concatenate(pieces, axis=0).astype(BF16)


def own_body(weights, x, block, table, out, padded):
    channels = x.shape[0]
    padded[...] = jnp.zeros_like(padded)
    padded[0:channels, :] = x[...]
    grid = silu(
        lax.dot_general(
            padded[...], weights[:, 0:WIDE], (((0,), (1,)), ((), ())), preferred_element_type=F32
        )
    ).astype(BF16)
    out[...] = grid.astype(F32) + mul(table[...], block[...])


def local_body(latent, message, neighbours, out):
    nodes = latent.shape[0]
    count = neighbours.shape[0]
    spare = jnp.zeros((8 - count, nodes), jnp.int32)
    ids = jnp.concatenate([neighbours[...], spare], axis=0).T
    node = lax.broadcasted_iota(jnp.int32, (nodes, nodes), 1)
    table = jnp.where(node == ids[:, 0:1], 1.0, 0.0)
    for k in range(1, count):
        table += jnp.where(node == ids[:, k : k + 1], 1.0, 0.0)
    out[...] = latent[...].astype(F32) + mul(table.astype(BF16), message[...])


def decode_body(here, base, far_ids, arrived, weights, out):
    nodes, channels = base.shape
    w_dec = weights[:, WIDE + 2 * channels :]
    hot = far_table(far_ids, here[0], -1, nodes)
    after = (base[...] + mul_tn(hot, arrived[...])).astype(BF16)
    out[...] = silu(mul_nt(after, w_dec)).astype(BF16)


def add_body(before, *rest):
    *blocks, table, out, joined = rest
    nodes = blocks[0].shape[0]
    for i, block in enumerate(blocks):
        joined[i * nodes : (i + 1) * nodes, :] = block[...]
    out[...] = (before[...].astype(F32) + mul(table[...], joined[...])).astype(out.dtype)


def call(body, out_shape, args, scratch=(), name=None, stored=(), far_off=()):
    near = len(args)
    last = near + len(stored)
    args = (*args, *stored, *far_off)
    hbm = pl.BlockSpec(memory_space=pltpu.HBM)
    smem = pl.BlockSpec(memory_space=pltpu.SMEM)
    vmem = pl.BlockSpec(memory_space=pltpu.VMEM)
    many = isinstance(out_shape, (list, tuple))
    args = [
        a if a.ndim == 1 else pltpu.with_memory_space_constraint(a, place)
        for a, place in zip(args, [pltpu.VMEM] * near + [pltpu.HBM] * (len(args) - near))
    ]
    return pl.pallas_call(
        body,
        out_shape=out_shape,
        in_specs=[
            smem if a.ndim == 1 else hbm if i >= last else vmem for i, a in enumerate(args)
        ],
        out_specs=[vmem for _ in out_shape] if many else vmem,
        scratch_shapes=scratch,
        compiler_params=VMEM,
        name=name,
    )(*args)


def shape(*dims, kind=BF16):
    return pltpu.VMEM(dims, kind)


def far_exchange(rows):
    patches, chans = lax.axis_size("patch"), lax.axis_size("chan")
    kinds = len(FAR[0])
    count, channels = rows.shape
    each = count // (chans * kinds)
    mine = lax.all_to_all(
        rows.reshape(chans, kinds * each, channels), "chan", 0, 0, tiled=True
    ).reshape(chans, kinds, each, channels)
    arrived = []
    for kind in range(kinds):
        pairs = []
        for c in range(chans):
            if FAR[c][kind] is None:
                continue
            for p in range(patches):
                pairs.append((p * chans + c, (p + FAR[c][kind]) % patches * chans + c))
        arrived.append(lax.ppermute(mine[:, kind], ("patch", "chan"), pairs))
    back = jnp.stack(arrived, axis=1).reshape(chans, kinds * each, channels)
    return lax.all_to_all(back, "chan", 0, 0, tiled=True).reshape(count, channels)


def shards(
    grid_in,
    mesh_embed,
    w_embed,
    w_edge,
    w_proc,
    w_dec,
    pack_rows,
    recv_node,
    far_send,
    far_recv,
    loc_nbr,
    dec_edge,
):
    patch = lax.axis_index("patch").astype(jnp.int32)
    here = patch.reshape(1)
    core = (patch % 2).reshape(1)
    channels = mesh_embed.shape[1]
    nodes = mesh_embed.shape[0]
    rows = grid_in.shape[0]
    offsets, slots = pack_rows.shape[2:]
    x = grid_in.T
    pack = pack_rows.reshape(offsets, 1, slots)
    recv = recv_node.reshape(offsets, 1, slots)
    far_out_ids = far_send.reshape(far_send.shape[2:]).T
    far_in_ids = far_recv.reshape(far_recv.shape[2:]).T
    def stored(*dims):
        return pltpu.HBM(dims, BF16)

    def work(blocks):
        wide = pltpu.VMEM((channels, blocks * slots), BF16)
        return wide, wide, pltpu.VMEM((nodes, blocks * slots), BF16)

    block = shape(SENT, slots)
    pair = shape(2, SENT, slots)
    padded = pltpu.VMEM((SENT, rows), BF16)

    width = w_edge.shape[1]
    chans = lax.axis_size("chan")
    copies = call(
        weights_body,
        stored(chans, width, WIDE + 3 * channels),
        (),
        [pltpu.VMEM((WIDE, width), BF16)],
        name="weights",
        stored=(w_embed, w_edge, w_proc, w_dec),
    )
    copies, x, edges = lax.optimization_barrier((copies, x, dec_edge.T))
    weights = lax.all_to_all(copies, "chan", 0, 0, tiled=True).reshape(chans * width, -1)
    three, up, down, own = call(
        pack_body,
        [block, pair, pair, block],
        (core,),
        [pltpu.VMEM((rows, 2 * slots), BF16)],
        name="pack",
        stored=(x, pack),
    )
    three = by_core(three, -3, 3)
    up = shifted(up, 2)
    down = shifted(down, -2)
    own_table, near_table, late_table = call(
        tables_body,
        [stored(rows, n * nodes) for n in (1, 3, 3)],
        (core,),
        name="tables",
        stored=(edges,),
    )
    up, down, three, own_table = lax.optimization_barrier((up, down, three, own_table))
    sib = by_core(jnp.stack([own, up[1], down[1]]), 1, -1)
    early = call(
        early_body,
        shape(nodes, channels, kind=F32),
        (core, x, pack, up, down, three, weights, recv),
        [*work(4), padded, pltpu.VMEM((nodes, channels), BF16), pltpu.SemaphoreType.DMA],
        name="early",
        far_off=(mesh_embed,),
    )
    mesh_latent, node_msg, far_sent = call(
        encode_body,
        [stored(nodes, channels), stored(nodes, channels), shape(8 * 16, channels)],
        (core, here, early, sib, weights, recv, far_out_ids),
        [*work(3)],
        name="encode",
    )
    base = call(
        local_body,
        shape(nodes, channels, kind=F32),
        (),
        name="short",
        stored=(mesh_latent, node_msg, loc_nbr.T),
    )
    arrived = far_exchange(far_sent)
    dec_msg = call(
        decode_body,
        shape(nodes, channels),
        (here, base, far_in_ids, arrived, weights),
        name="decode",
    )

    def added(name, before, blocks, table, kind=F32):
        return call(
            add_body,
            shape(rows, channels, kind=kind) if kind == F32 else stored(rows, channels),
            (before, *blocks, table),
            [pltpu.VMEM((len(blocks) * nodes, channels), BF16)],
            name=name,
        )

    second = by_core(dec_msg, 2, -2)
    first = by_core(dec_msg, -2, 2)
    sib = by_core(dec_msg, 1, -1)
    total = call(
        own_body,
        shape(rows, channels, kind=F32),
        (weights, x, dec_msg, own_table),
        [pltpu.VMEM((WIDE, rows), BF16)],
        name="own",
    )
    first, total = lax.optimization_barrier((first, total))
    three = by_core(first, -1, 1)
    relay_first = by_core(first, 1, -1)
    relay_second = by_core(second, 1, -1)
    total = added("near", total, (sib, first, second), near_table)
    return added("collect", total, (three, relay_first, relay_second), late_table, BF16)


def solution(mesh):
    both = P(("patch", "chan"), None)
    column = P(None, "chan")
    lists = P("patch", "chan", None, None)
    in_specs = (both, both, column, column, column, column, lists, lists, lists, lists, both, both)
    return jax.shard_map(shards, mesh=mesh, in_specs=in_specs, out_specs=both, check_vma=False)
```

```python
import functools

import jax
import jax.numpy as jnp
from jax import lax
from jax.experimental import pallas as pl
from jax.experimental.pallas import tpu as pltpu
from jax.sharding import PartitionSpec as P

BF16 = jnp.bfloat16
F32 = jnp.float32
SENT = 240
WIDE = 256
FAR = ((None, 2, 1, 16), (None, -2, -1, -16), (64, 32, 4, 8), (None, -32, -4, -8))
VMEM = pltpu.CompilerParams(vmem_limit_bytes=20 * 1024 * 1024)


def silu(v):
    h = 0.5 * v
    return h + h * jnp.tanh(h)


def mul(a, b):
    return jnp.dot(a, b, preferred_element_type=F32)


def mul_nt(a, b):
    return lax.dot_general(a, b, (((1,), (1,)), ((), ())), preferred_element_type=F32)


def mul_tn(a, b):
    return lax.dot_general(a, b, (((0,), (0,)), ((), ())), preferred_element_type=F32)


def shifted(value, steps):
    count = lax.axis_size("patch")
    return lax.ppermute(value, "patch", [(i, (i + steps) % count) for i in range(count)])


def by_core(value, even_steps, odd_steps):
    count = lax.axis_size("patch")
    pairs = [(i, (i + (even_steps if i % 2 == 0 else odd_steps)) % count) for i in range(count)]
    return lax.ppermute(value, "patch", pairs)


def silu_rows(weights, block):
    return silu(mul(weights, block)).astype(BF16)


def one_hot(where, ids):
    same = where == jnp.broadcast_to(ids.astype(jnp.int16), where.shape)
    return jnp.where(same, jnp.ones(where.shape, BF16), jnp.zeros(where.shape, BF16))


def positions(dims, axis):
    return lax.broadcasted_iota(jnp.int32, dims, axis).astype(jnp.int16)


def pack_body(core, x, pack, three, up, down, own, hot):
    here = core[0]
    channels, rows = x.shape
    slots = pack.shape[-1]
    row_of = positions((rows, slots), 0)
    last = channels // 16 * 16
    blank = jnp.zeros((SENT - last, slots), BF16)

    def chosen(outs, offsets):
        for i, offset in enumerate(offsets):
            hot[:, i * slots : (i + 1) * slots] = one_hot(row_of, pack[offset])
        found = mul(x[...], hot[...]).astype(BF16)
        for i, out in enumerate(outs):
            out[last:SENT, :] = blank
            out[0:channels, :] = found[:, i * slots : (i + 1) * slots]

    chosen((up.at[0], up.at[1]), (5, jnp.where(here == 0, 6, 4)))
    chosen((down.at[0], down.at[1]), (1, jnp.where(here == 0, 2, 0)))
    chosen((three, own), (jnp.where(here == 0, 0, 6), jnp.where(here == 0, 4, 2)))


def weights_body(embed, edge, proc, dec, out, padded):
    copies, width, columns = out.shape
    eye = one_hot(
        positions((width, width), 0), lax.broadcasted_iota(jnp.int32, (width, width), 1)
    )
    padded[...] = jnp.zeros_like(padded)
    padded[0 : embed.shape[0], :] = embed[...]
    at = 0
    for piece in (padded, edge, proc, dec):
        turned = mul_nt(eye, piece[...]).astype(BF16)
        for i in range(copies):
            out[i, :, at : at + piece.shape[0]] = turned
        at += piece.shape[0]


def tables_body(core, edges, *tables):
    is_even = core[0] == 0
    rows = edges.shape[1]
    order = (
        3,
        jnp.where(is_even, 4, 2),
        jnp.where(is_even, 5, 1),
        jnp.where(is_even, 1, 5),
        jnp.where(is_even, 0, 6),
        jnp.where(is_even, 2, 4),
        jnp.where(is_even, 6, 0),
    )
    count = edges.shape[0]
    spare = jnp.zeros((8 - count, rows), jnp.int32)
    ids = jnp.concatenate([edges[...], spare], axis=0).T
    nodes = sum(table.shape[1] for table in tables) // len(order)
    step = 128
    columns = positions((step, step), 1)
    for first in range(0, rows, step):
        wide = [
            jnp.broadcast_to(ids[first : first + step, k : k + 1], (step, step))
            for k in range(count)
        ]
        at = 0
        for table in tables:
            for block in range(table.shape[1] // nodes):
                base = order[at] * nodes
                moved = [(w - base).astype(jnp.int16) for w in wide]
                at += 1
                for part in range(0, nodes, step):
                    here = columns + jnp.int16(part)
                    total = one_hot(here, moved[0])
                    for k in range(1, count):
                        total += one_hot(here, moved[k])
                    left = block * nodes + part
                    table[first : first + step, left : left + step] = total


def messages(blocks, w_embed, w_edge, rows, sent):
    slots = blocks[0].shape[1]
    for i, block in enumerate(blocks):
        rows[:, i * slots : (i + 1) * slots] = silu_rows(w_embed, block)
    for i in range(len(blocks)):
        at = slice(i * slots, (i + 1) * slots)
        sent[:, at] = silu_rows(w_edge, rows[:, at])


def receivers(recv, offsets, hot):
    nodes, slots = hot.shape[0], recv.shape[-1]
    node_of = positions((nodes, slots), 0)
    for i, offset in enumerate(offsets):
        hot[:, i * slots : (i + 1) * slots] = one_hot(node_of, recv[offset])


def early_body(
    core, x, pack, up, down, three, weights, recv, embed, out, rows, sent, hot, padded, near, arrived
):
    is_even = core[0] == 0
    nodes, channels = embed.shape
    fetch = pltpu.make_async_copy(embed, near, arrived)
    fetch.start()
    slots = recv.shape[-1]
    w_embed = weights[:, 0:SENT]
    w_edge = weights[:, WIDE : WIDE + channels]
    padded[...] = jnp.zeros_like(padded)
    padded[0 : x.shape[0], :] = x[...]
    local = mul(padded[...], one_hot(positions((x.shape[1], slots), 0), pack[3])).astype(BF16)
    messages((local, up[0], down[0], three[...]), w_embed, w_edge, rows, sent)
    receivers(recv, (3, 5, 1, jnp.where(is_even, 6, 0)), hot)
    total = mul_nt(hot[...], sent[...])
    fetch.wait()
    out[...] = near[...].astype(F32) + total


def encode_body(
    core, here, early, sib, weights, recv, far_ids, latent, message, far, rows, sent, hot, w_proc
):
    is_even = core[0] == 0
    nodes, channels = early.shape
    w_embed = weights[:, 0:SENT]
    w_edge = weights[:, WIDE : WIDE + channels]
    w_proc[...] = weights[:, WIDE + channels : WIDE + 2 * channels]
    messages((sib[0], sib[1], sib[2]), w_embed, w_edge, rows, sent)
    offsets = (jnp.where(is_even, 2, 4), jnp.where(is_even, 4, 6), jnp.where(is_even, 0, 2))
    receivers(recv, offsets, hot)
    rounded = (early[...] + mul_nt(hot[...], sent[...])).astype(BF16)
    latent[...] = rounded
    made = silu(mul_nt(rounded, w_proc[...])).astype(BF16)
    message[...] = made
    far[...] = mul(far_table(far_ids, here[0], 1, nodes), made).astype(BF16)


def far_table(ids, here, sign, nodes):
    count = ids.shape[1]
    column = lax.broadcasted_iota(jnp.int32, ids.shape, 1)
    node = lax.broadcasted_iota(jnp.int32, (ids.shape[0], nodes), 1)
    pieces = []
    for offset in sum(FAR, ()):
        if offset is None:
            pieces.append(jnp.zeros((ids.shape[0], nodes), F32))
            continue
        partner = lax.rem(here + sign * offset + count, count)
        chosen = jnp.sum(jnp.where(column == partner, ids[...], 0), axis=1, keepdims=True)
        pieces.append(jnp.where(node == chosen, 1.0, 0.0))
    return jnp.concatenate(pieces, axis=0).astype(BF16)


def own_body(weights, x, block, table, out, padded):
    channels = x.shape[0]
    padded[...] = jnp.zeros_like(padded)
    padded[0:channels, :] = x[...]
    grid = silu(
        lax.dot_general(
            padded[...], weights[:, 0:WIDE], (((0,), (1,)), ((), ())), preferred_element_type=F32
        )
    ).astype(BF16)
    out[...] = grid.astype(F32) + mul(table[...], block[...])


def local_body(latent, message, neighbours, out):
    nodes = latent.shape[0]
    count = neighbours.shape[0]
    spare = jnp.zeros((8 - count, nodes), jnp.int32)
    ids = jnp.concatenate([neighbours[...], spare], axis=0).T
    node = lax.broadcasted_iota(jnp.int32, (nodes, nodes), 1)
    table = jnp.where(node == ids[:, 0:1], 1.0, 0.0)
    for k in range(1, count):
        table += jnp.where(node == ids[:, k : k + 1], 1.0, 0.0)
    out[...] = latent[...].astype(F32) + mul(table.astype(BF16), message[...])


def decode_body(here, base, far_ids, arrived, weights, out):
    nodes, channels = base.shape
    w_dec = weights[:, WIDE + 2 * channels :]
    hot = far_table(far_ids, here[0], -1, nodes)
    after = (base[...] + mul_tn(hot, arrived[...])).astype(BF16)
    out[...] = silu(mul_nt(after, w_dec)).astype(BF16)


def add_body(before, *rest):
    *blocks, table, out, joined = rest
    nodes = blocks[0].shape[0]
    for i, block in enumerate(blocks):
        joined[i * nodes : (i + 1) * nodes, :] = block[...]
    out[...] = before[...] + mul(table[...], joined[...])


def collect_body(before, *rest):
    *blocks, table, out, joined, done, left = rest
    nodes = blocks[0].shape[0]
    for i, block in enumerate(blocks):
        joined[i * nodes : (i + 1) * nodes, :] = block[...]
    step = out.shape[0] // 4
    stores = []
    for i in range(4):
        at = pl.ds(i * step, step)
        done[at, :] = (before[at, :] + mul(table[at, :], joined[...])).astype(BF16)
        stores.append(pltpu.make_async_copy(done.at[at, :], out.at[at, :], left.at[i]))
        stores[-1].start()
    for store in stores:
        store.wait()


def call(body, out_shape, args, scratch=(), name=None, stored=(), far_off=(), keeps=0):
    near = len(args)
    last = near + len(stored)
    args = (*args, *stored, *far_off)
    hbm = pl.BlockSpec(memory_space=pltpu.HBM)
    smem = pl.BlockSpec(memory_space=pltpu.SMEM)
    vmem = pl.BlockSpec(memory_space=pltpu.VMEM)
    many = isinstance(out_shape, (list, tuple))
    args = [
        a if a.ndim == 1 else pltpu.with_memory_space_constraint(a, place)
        for a, place in zip(args, [pltpu.VMEM] * near + [pltpu.HBM] * (len(args) - near))
    ]
    return pl.pallas_call(
        body,
        out_shape=out_shape,
        in_specs=[
            smem if a.ndim == 1 else hbm if i >= last else vmem for i, a in enumerate(args)
        ],
        out_specs=[vmem for _ in out_shape] if many else hbm if keeps else vmem,
        scratch_shapes=scratch,
        compiler_params=VMEM,
        name=name,
    )(*args)


def shape(*dims, kind=BF16):
    return pltpu.VMEM(dims, kind)


def far_exchange(rows):
    patches, chans = lax.axis_size("patch"), lax.axis_size("chan")
    kinds = len(FAR[0])
    count, channels = rows.shape
    each = count // (chans * kinds)
    mine = lax.all_to_all(
        rows.reshape(chans, kinds * each, channels), "chan", 0, 0, tiled=True
    ).reshape(chans, kinds, each, channels)
    arrived = []
    for kind in range(kinds):
        pairs = []
        for c in range(chans):
            if FAR[c][kind] is None:
                continue
            for p in range(patches):
                pairs.append((p * chans + c, (p + FAR[c][kind]) % patches * chans + c))
        arrived.append(lax.ppermute(mine[:, kind], ("patch", "chan"), pairs))
    back = jnp.stack(arrived, axis=1).reshape(chans, kinds * each, channels)
    return lax.all_to_all(back, "chan", 0, 0, tiled=True).reshape(count, channels)


def shards(
    grid_in,
    mesh_embed,
    w_embed,
    w_edge,
    w_proc,
    w_dec,
    pack_rows,
    recv_node,
    far_send,
    far_recv,
    loc_nbr,
    dec_edge,
):
    patch = lax.axis_index("patch").astype(jnp.int32)
    here = patch.reshape(1)
    core = (patch % 2).reshape(1)
    channels = mesh_embed.shape[1]
    nodes = mesh_embed.shape[0]
    rows = grid_in.shape[0]
    offsets, slots = pack_rows.shape[2:]
    x = grid_in.T
    pack = pack_rows.reshape(offsets, 1, slots)
    recv = recv_node.reshape(offsets, 1, slots)
    far_out_ids = far_send.reshape(far_send.shape[2:]).T
    far_in_ids = far_recv.reshape(far_recv.shape[2:]).T
    def stored(*dims):
        return pltpu.HBM(dims, BF16)

    def work(blocks):
        wide = pltpu.VMEM((channels, blocks * slots), BF16)
        return wide, wide, pltpu.VMEM((nodes, blocks * slots), BF16)

    block = shape(SENT, slots)
    pair = shape(2, SENT, slots)
    padded = pltpu.VMEM((SENT, rows), BF16)

    width = w_edge.shape[1]
    chans = lax.axis_size("chan")
    copies = call(
        weights_body,
        stored(chans, width, WIDE + 3 * channels),
        (),
        [pltpu.VMEM((WIDE, width), BF16)],
        name="weights",
        stored=(w_embed, w_edge, w_proc, w_dec),
    )
    copies, x, edges = lax.optimization_barrier((copies, x, dec_edge.T))
    weights = lax.all_to_all(copies, "chan", 0, 0, tiled=True).reshape(chans * width, -1)
    three, up, down, own = call(
        pack_body,
        [block, pair, pair, block],
        (core,),
        [pltpu.VMEM((rows, 2 * slots), BF16)],
        name="pack",
        stored=(x, pack),
    )
    three = by_core(three, -3, 3)
    up = shifted(up, 2)
    down = shifted(down, -2)
    own_table, near_table, late_table = call(
        tables_body,
        [stored(rows, n * nodes) for n in (1, 3, 3)],
        (core,),
        name="tables",
        stored=(edges,),
    )
    three, up, own_table = lax.optimization_barrier((three, up, own_table))
    up, down = lax.optimization_barrier((up, down))
    sib = by_core(jnp.stack([own, up[1], down[1]]), 1, -1)
    early = call(
        early_body,
        shape(nodes, channels, kind=F32),
        (core, x, pack, up, down, three, weights, recv),
        [*work(4), padded, pltpu.VMEM((nodes, channels), BF16), pltpu.SemaphoreType.DMA],
        name="early",
        far_off=(mesh_embed,),
    )
    mesh_latent, node_msg, far_sent = call(
        encode_body,
        [stored(nodes, channels), stored(nodes, channels), shape(8 * 16, channels)],
        (core, here, early, sib, weights, recv, far_out_ids),
        [*work(3), pltpu.VMEM((channels, channels), BF16)],
        name="encode",
    )
    base = call(
        local_body,
        shape(nodes, channels, kind=F32),
        (),
        name="short",
        stored=(mesh_latent, node_msg, loc_nbr.T),
    )
    arrived = far_exchange(far_sent)
    dec_msg = call(
        decode_body,
        shape(nodes, channels),
        (here, base, far_in_ids, arrived, weights),
        name="decode",
    )

    def added(name, before, blocks, table):
        return call(
            add_body,
            shape(rows, channels, kind=F32),
            (before, *blocks, table),
            [pltpu.VMEM((len(blocks) * nodes, channels), BF16)],
            name=name,
        )

    second = by_core(dec_msg, 2, -2)
    first = by_core(dec_msg, -2, 2)
    sib = by_core(dec_msg, 1, -1)
    total = call(
        own_body,
        shape(rows, channels, kind=F32),
        (weights, x, dec_msg, own_table),
        [pltpu.VMEM((WIDE, rows), BF16)],
        name="own",
    )
    first, total = lax.optimization_barrier((first, total))
    three = by_core(first, -1, 1)
    relay_first = by_core(first, 1, -1)
    relay_second = by_core(second, 1, -1)
    total = added("near", total, (sib, first, second), near_table)
    return call(
        collect_body,
        stored(rows, channels),
        (total, three, relay_first, relay_second, late_table),
        [
            pltpu.VMEM((3 * nodes, channels), BF16),
            pltpu.VMEM((rows, channels), BF16),
            pltpu.SemaphoreType.DMA((4,)),
        ],
        name="collect",
        keeps=1,
    )


def solution(mesh):
    both = P(("patch", "chan"), None)
    column = P(None, "chan")
    lists = P("patch", "chan", None, None)
    in_specs = (both, both, column, column, column, column, lists, lists, lists, lists, both, both)
    return jax.shard_map(shards, mesh=mesh, in_specs=in_specs, out_specs=both, check_vma=False)
```

```python
import functools

import jax
import jax.numpy as jnp
from jax import lax
from jax.experimental import pallas as pl
from jax.experimental.pallas import tpu as pltpu
from jax.sharding import PartitionSpec as P

BF16 = jnp.bfloat16
F32 = jnp.float32
SENT = 240
WIDE = 256
FAR = ((None, 2, 1, 16), (None, -2, -1, -16), (64, 32, 4, 8), (None, -32, -4, -8))
VMEM = pltpu.CompilerParams(vmem_limit_bytes=20 * 1024 * 1024)


def silu(v):
    h = 0.5 * v
    return h + h * jnp.tanh(h)


def mul(a, b):
    return jnp.dot(a, b, preferred_element_type=F32)


def mul_nt(a, b):
    return lax.dot_general(a, b, (((1,), (1,)), ((), ())), preferred_element_type=F32)


def mul_tn(a, b):
    return lax.dot_general(a, b, (((0,), (0,)), ((), ())), preferred_element_type=F32)


def shifted(value, steps):
    count = lax.axis_size("patch")
    return lax.ppermute(value, "patch", [(i, (i + steps) % count) for i in range(count)])


def by_core(value, even_steps, odd_steps):
    count = lax.axis_size("patch")
    pairs = [(i, (i + (even_steps if i % 2 == 0 else odd_steps)) % count) for i in range(count)]
    return lax.ppermute(value, "patch", pairs)


def silu_rows(weights, block):
    return silu(mul(weights, block)).astype(BF16)


def one_hot(where, ids):
    same = where == jnp.broadcast_to(ids.astype(jnp.int16), where.shape)
    return jnp.where(same, jnp.ones(where.shape, BF16), jnp.zeros(where.shape, BF16))


def positions(dims, axis):
    return lax.broadcasted_iota(jnp.int32, dims, axis).astype(jnp.int16)


def pack_body(core, x, pack, three, up, down, own, hot):
    here = core[0]
    channels, rows = x.shape
    slots = pack.shape[-1]
    row_of = positions((rows, slots), 0)
    last = channels // 16 * 16
    blank = jnp.zeros((SENT - last, slots), BF16)

    def chosen(outs, offsets):
        for i, offset in enumerate(offsets):
            hot[:, i * slots : (i + 1) * slots] = one_hot(row_of, pack[offset])
        found = mul(x[...], hot[...]).astype(BF16)
        for i, out in enumerate(outs):
            out[last:SENT, :] = blank
            out[0:channels, :] = found[:, i * slots : (i + 1) * slots]

    chosen((up.at[0], up.at[1]), (5, jnp.where(here == 0, 6, 4)))
    chosen((down.at[0], down.at[1]), (1, jnp.where(here == 0, 2, 0)))
    chosen((three, own), (jnp.where(here == 0, 0, 6), jnp.where(here == 0, 4, 2)))


def weights_body(embed, edge, proc, dec, out, padded):
    copies, width, columns = out.shape
    eye = one_hot(
        positions((width, width), 0), lax.broadcasted_iota(jnp.int32, (width, width), 1)
    )
    padded[...] = jnp.zeros_like(padded)
    padded[0 : embed.shape[0], :] = embed[...]
    at = 0
    for piece in (padded, edge, proc, dec):
        turned = mul_nt(eye, piece[...]).astype(BF16)
        for i in range(copies):
            out[i, :, at : at + piece.shape[0]] = turned
        at += piece.shape[0]


def tables_body(core, edges, *tables):
    is_even = core[0] == 0
    rows = edges.shape[1]
    order = (
        3,
        jnp.where(is_even, 4, 2),
        jnp.where(is_even, 5, 1),
        jnp.where(is_even, 1, 5),
        jnp.where(is_even, 0, 6),
        jnp.where(is_even, 2, 4),
        jnp.where(is_even, 6, 0),
    )
    count = edges.shape[0]
    spare = jnp.zeros((8 - count, rows), jnp.int32)
    ids = jnp.concatenate([edges[...], spare], axis=0).T
    nodes = sum(table.shape[1] for table in tables) // len(order)
    step = 128
    columns = positions((step, step), 1)
    for first in range(0, rows, step):
        wide = [
            jnp.broadcast_to(ids[first : first + step, k : k + 1], (step, step))
            for k in range(count)
        ]
        at = 0
        for table in tables:
            for block in range(table.shape[1] // nodes):
                base = order[at] * nodes
                moved = [(w - base).astype(jnp.int16) for w in wide]
                at += 1
                for part in range(0, nodes, step):
                    here = columns + jnp.int16(part)
                    total = one_hot(here, moved[0])
                    for k in range(1, count):
                        total += one_hot(here, moved[k])
                    left = block * nodes + part
                    table[first : first + step, left : left + step] = total


def messages(blocks, w_embed, w_edge, rows, sent):
    slots = blocks[0].shape[1]
    for i, block in enumerate(blocks):
        rows[:, i * slots : (i + 1) * slots] = silu_rows(w_embed, block)
    for i in range(len(blocks)):
        at = slice(i * slots, (i + 1) * slots)
        sent[:, at] = silu_rows(w_edge, rows[:, at])


def receivers(recv, offsets, hot):
    nodes, slots = hot.shape[0], recv.shape[-1]
    node_of = positions((nodes, slots), 0)
    for i, offset in enumerate(offsets):
        hot[:, i * slots : (i + 1) * slots] = one_hot(node_of, recv[offset])


def early_body(
    core, x, pack, up, down, three, weights, recv, embed, out, rows, sent, hot, padded, near, arrived
):
    is_even = core[0] == 0
    nodes, channels = embed.shape
    fetch = pltpu.make_async_copy(embed, near, arrived)
    fetch.start()
    slots = recv.shape[-1]
    w_embed = weights[:, 0:SENT]
    w_edge = weights[:, WIDE : WIDE + channels]
    padded[...] = jnp.zeros_like(padded)
    padded[0 : x.shape[0], :] = x[...]
    local = mul(padded[...], one_hot(positions((x.shape[1], slots), 0), pack[3])).astype(BF16)
    messages((local, up[0], down[0], three[...]), w_embed, w_edge, rows, sent)
    receivers(recv, (3, 5, 1, jnp.where(is_even, 6, 0)), hot)
    total = mul_nt(hot[...], sent[...])
    fetch.wait()
    out[...] = near[...].astype(F32) + total


def encode_body(
    core, here, early, sib, weights, recv, far_ids, latent, message, far, rows, sent, hot, w_proc
):
    is_even = core[0] == 0
    nodes, channels = early.shape
    w_embed = weights[:, 0:SENT]
    w_edge = weights[:, WIDE : WIDE + channels]
    w_proc[...] = weights[:, WIDE + channels : WIDE + 2 * channels]
    messages((sib[0], sib[1], sib[2]), w_embed, w_edge, rows, sent)
    offsets = (jnp.where(is_even, 2, 4), jnp.where(is_even, 4, 6), jnp.where(is_even, 0, 2))
    receivers(recv, offsets, hot)
    rounded = (early[...] + mul_nt(hot[...], sent[...])).astype(BF16)
    latent[...] = rounded
    made = silu(mul_nt(rounded, w_proc[...])).astype(BF16)
    message[...] = made
    far[...] = mul(far_table(far_ids, here[0], 1, nodes), made).astype(BF16)


def far_table(ids, here, sign, nodes):
    count = ids.shape[1]
    column = lax.broadcasted_iota(jnp.int32, ids.shape, 1)
    node = lax.broadcasted_iota(jnp.int32, (ids.shape[0], nodes), 1)
    pieces = []
    for offset in sum(FAR, ()):
        if offset is None:
            pieces.append(jnp.zeros((ids.shape[0], nodes), F32))
            continue
        partner = lax.rem(here + sign * offset + count, count)
        chosen = jnp.sum(jnp.where(column == partner, ids[...], 0), axis=1, keepdims=True)
        pieces.append(jnp.where(node == chosen, 1.0, 0.0))
    return jnp.concatenate(pieces, axis=0).astype(BF16)


def own_body(weights, x, block, table, out, padded):
    channels = x.shape[0]
    padded[...] = jnp.zeros_like(padded)
    padded[0:channels, :] = x[...]
    grid = silu(
        lax.dot_general(
            padded[...], weights[:, 0:WIDE], (((0,), (1,)), ((), ())), preferred_element_type=F32
        )
    ).astype(BF16)
    out[...] = grid.astype(F32) + mul(table[...], block[...])


def local_body(latent, message, neighbours, out):
    nodes = latent.shape[0]
    count = neighbours.shape[0]
    spare = jnp.zeros((8 - count, nodes), jnp.int32)
    ids = jnp.concatenate([neighbours[...], spare], axis=0).T
    node = lax.broadcasted_iota(jnp.int32, (nodes, nodes), 1)
    table = jnp.where(node == ids[:, 0:1], 1.0, 0.0)
    for k in range(1, count):
        table += jnp.where(node == ids[:, k : k + 1], 1.0, 0.0)
    out[...] = latent[...].astype(F32) + mul(table.astype(BF16), message[...])


def decode_body(here, base, far_ids, arrived, weights, out):
    nodes, channels = base.shape
    w_dec = weights[:, WIDE + 2 * channels :]
    hot = far_table(far_ids, here[0], -1, nodes)
    after = (base[...] + mul_tn(hot, arrived[...])).astype(BF16)
    out[...] = silu(mul_nt(after, w_dec)).astype(BF16)


def add_body(before, *rest):
    *blocks, table, out, joined = rest
    nodes = blocks[0].shape[0]
    for i, block in enumerate(blocks):
        joined[i * nodes : (i + 1) * nodes, :] = block[...]
    out[...] = before[...] + mul(table[...], joined[...])


def collect_body(before, *rest):
    *blocks, table, out, joined, done, left = rest
    nodes = blocks[0].shape[0]
    for i, block in enumerate(blocks):
        joined[i * nodes : (i + 1) * nodes, :] = block[...]
    step = out.shape[0] // 4
    stores = []
    for i in range(4):
        at = pl.ds(i * step, step)
        done[at, :] = (before[at, :] + mul(table[at, :], joined[...])).astype(BF16)
        stores.append(pltpu.make_async_copy(done.at[at, :], out.at[at, :], left.at[i]))
        stores[-1].start()
    for store in stores:
        store.wait()


def call(body, out_shape, args, scratch=(), name=None, stored=(), far_off=(), keeps=0):
    near = len(args)
    last = near + len(stored)
    args = (*args, *stored, *far_off)
    hbm = pl.BlockSpec(memory_space=pltpu.HBM)
    smem = pl.BlockSpec(memory_space=pltpu.SMEM)
    vmem = pl.BlockSpec(memory_space=pltpu.VMEM)
    many = isinstance(out_shape, (list, tuple))
    args = [
        a if a.ndim == 1 else pltpu.with_memory_space_constraint(a, place)
        for a, place in zip(args, [pltpu.VMEM] * near + [pltpu.HBM] * (len(args) - near))
    ]
    return pl.pallas_call(
        body,
        out_shape=out_shape,
        in_specs=[
            smem if a.ndim == 1 else hbm if i >= last else vmem for i, a in enumerate(args)
        ],
        out_specs=[vmem for _ in out_shape] if many else hbm if keeps else vmem,
        scratch_shapes=scratch,
        compiler_params=VMEM,
        name=name,
    )(*args)


def shape(*dims, kind=BF16):
    return pltpu.VMEM(dims, kind)


def far_exchange(rows):
    patches, chans = lax.axis_size("patch"), lax.axis_size("chan")
    kinds = len(FAR[0])
    count, channels = rows.shape
    each = count // (chans * kinds)
    mine = lax.all_to_all(
        rows.reshape(chans, kinds * each, channels), "chan", 0, 0, tiled=True
    ).reshape(chans, kinds, each, channels)
    arrived = []
    for kind in range(kinds):
        pairs = []
        for c in range(chans):
            if FAR[c][kind] is None:
                continue
            for p in range(patches):
                pairs.append((p * chans + c, (p + FAR[c][kind]) % patches * chans + c))
        arrived.append(lax.ppermute(mine[:, kind], ("patch", "chan"), pairs))
    back = jnp.stack(arrived, axis=1).reshape(chans, kinds * each, channels)
    return lax.all_to_all(back, "chan", 0, 0, tiled=True).reshape(count, channels)


def shards(
    grid_in,
    mesh_embed,
    w_embed,
    w_edge,
    w_proc,
    w_dec,
    pack_rows,
    recv_node,
    far_send,
    far_recv,
    loc_nbr,
    dec_edge,
):
    patch = lax.axis_index("patch").astype(jnp.int32)
    here = patch.reshape(1)
    core = (patch % 2).reshape(1)
    channels = mesh_embed.shape[1]
    nodes = mesh_embed.shape[0]
    rows = grid_in.shape[0]
    offsets, slots = pack_rows.shape[2:]
    x = grid_in.T
    pack = pack_rows.reshape(offsets, 1, slots)
    recv = recv_node.reshape(offsets, 1, slots)
    far_out_ids = far_send.reshape(far_send.shape[2:]).T
    far_in_ids = far_recv.reshape(far_recv.shape[2:]).T
    def stored(*dims):
        return pltpu.HBM(dims, BF16)

    def work(blocks):
        wide = pltpu.VMEM((channels, blocks * slots), BF16)
        return wide, wide, pltpu.VMEM((nodes, blocks * slots), BF16)

    block = shape(SENT, slots)
    pair = shape(2, SENT, slots)
    padded = pltpu.VMEM((SENT, rows), BF16)

    width = w_edge.shape[1]
    chans = lax.axis_size("chan")
    copies = call(
        weights_body,
        stored(chans, width, WIDE + 3 * channels),
        (),
        [pltpu.VMEM((WIDE, width), BF16)],
        name="weights",
        stored=(w_embed, w_edge, w_proc, w_dec),
    )
    copies, x, edges = lax.optimization_barrier((copies, x, dec_edge.T))
    weights = lax.all_to_all(copies, "chan", 0, 0, tiled=True).reshape(chans * width, -1)
    three, up, down, own = call(
        pack_body,
        [block, pair, pair, block],
        (core, x, pack),
        [pltpu.VMEM((rows, 2 * slots), BF16)],
        name="pack",
    )
    three = by_core(three, -3, 3)
    up = shifted(up, 2)
    down = shifted(down, -2)
    own_table, near_table, late_table = call(
        tables_body,
        [stored(rows, n * nodes) for n in (1, 3, 3)],
        (core,),
        name="tables",
        stored=(edges,),
    )
    three, up, own_table = lax.optimization_barrier((three, up, own_table))
    up, down = lax.optimization_barrier((up, down))
    sib = by_core(jnp.stack([own, up[1], down[1]]), 1, -1)
    early = call(
        early_body,
        shape(nodes, channels, kind=F32),
        (core, x, pack, up, down, three, weights, recv),
        [*work(4), padded, pltpu.VMEM((nodes, channels), BF16), pltpu.SemaphoreType.DMA],
        name="early",
        far_off=(mesh_embed,),
    )
    mesh_latent, node_msg, far_sent = call(
        encode_body,
        [stored(nodes, channels), stored(nodes, channels), shape(8 * 16, channels)],
        (core, here, early, sib, weights, recv, far_out_ids),
        [*work(3), pltpu.VMEM((channels, channels), BF16)],
        name="encode",
    )
    base = call(
        local_body,
        shape(nodes, channels, kind=F32),
        (),
        name="short",
        stored=(mesh_latent, node_msg, loc_nbr.T),
    )
    arrived = far_exchange(far_sent)
    dec_msg = call(
        decode_body,
        shape(nodes, channels),
        (here, base, far_in_ids, arrived, weights),
        name="decode",
    )

    def added(name, before, blocks, table):
        return call(
            add_body,
            shape(rows, channels, kind=F32),
            (before, *blocks, table),
            [pltpu.VMEM((len(blocks) * nodes, channels), BF16)],
            name=name,
        )

    second = by_core(dec_msg, 2, -2)
    first = by_core(dec_msg, -2, 2)
    sib = by_core(dec_msg, 1, -1)
    total = call(
        own_body,
        shape(rows, channels, kind=F32),
        (weights, x, dec_msg, own_table),
        [pltpu.VMEM((WIDE, rows), BF16)],
        name="own",
    )
    first, total = lax.optimization_barrier((first, total))
    three = by_core(first, -1, 1)
    relay_first = by_core(first, 1, -1)
    relay_second = by_core(second, 1, -1)
    total = added("near", total, (sib, first, second), near_table)
    return call(
        collect_body,
        stored(rows, channels),
        (total, three, relay_first, relay_second, late_table),
        [
            pltpu.VMEM((3 * nodes, channels), BF16),
            pltpu.VMEM((rows, channels), BF16),
            pltpu.SemaphoreType.DMA((4,)),
        ],
        name="collect",
        keeps=1,
    )


def solution(mesh):
    both = P(("patch", "chan"), None)
    column = P(None, "chan")
    lists = P("patch", "chan", None, None)
    in_specs = (both, both, column, column, column, column, lists, lists, lists, lists, both, both)
    return jax.shard_map(shards, mesh=mesh, in_specs=in_specs, out_specs=both, check_vma=False)
```

```python
import functools

import jax
import jax.numpy as jnp
from jax import lax
from jax.experimental import pallas as pl
from jax.experimental.pallas import tpu as pltpu
from jax.sharding import PartitionSpec as P

BF16 = jnp.bfloat16
F32 = jnp.float32
SENT = 240
WIDE = 256
FAR = ((None, 2, 1, 16), (None, -2, -1, -16), (64, 32, 4, 8), (None, -32, -4, -8))
VMEM = pltpu.CompilerParams(vmem_limit_bytes=20 * 1024 * 1024)


def silu(v):
    h = 0.5 * v
    return h + h * jnp.tanh(h)


def mul(a, b):
    return jnp.dot(a, b, preferred_element_type=F32)


def mul_nt(a, b):
    return lax.dot_general(a, b, (((1,), (1,)), ((), ())), preferred_element_type=F32)


def mul_tn(a, b):
    return lax.dot_general(a, b, (((0,), (0,)), ((), ())), preferred_element_type=F32)


def shifted(value, steps):
    count = lax.axis_size("patch")
    return lax.ppermute(value, "patch", [(i, (i + steps) % count) for i in range(count)])


def by_core(value, even_steps, odd_steps):
    count = lax.axis_size("patch")
    pairs = [(i, (i + (even_steps if i % 2 == 0 else odd_steps)) % count) for i in range(count)]
    return lax.ppermute(value, "patch", pairs)


def silu_rows(weights, block):
    return silu(mul(weights, block)).astype(BF16)


def one_hot(where, ids):
    same = where == jnp.broadcast_to(ids.astype(jnp.int16), where.shape)
    return jnp.where(same, jnp.ones(where.shape, BF16), jnp.zeros(where.shape, BF16))


def positions(dims, axis):
    return lax.broadcasted_iota(jnp.int32, dims, axis).astype(jnp.int16)


def pack_body(core, x, pack, three, up, down, own, hot):
    here = core[0]
    channels, rows = x.shape
    slots = pack.shape[-1]
    row_of = positions((rows, slots), 0)
    last = channels // 16 * 16
    blank = jnp.zeros((SENT - last, slots), BF16)

    def chosen(outs, offsets):
        for i, offset in enumerate(offsets):
            hot[:, i * slots : (i + 1) * slots] = one_hot(row_of, pack[offset])
        found = mul(x[...], hot[...]).astype(BF16)
        for i, out in enumerate(outs):
            out[last:SENT, :] = blank
            out[0:channels, :] = found[:, i * slots : (i + 1) * slots]

    chosen((up.at[0], up.at[1]), (5, jnp.where(here == 0, 6, 4)))
    chosen((down.at[0], down.at[1]), (1, jnp.where(here == 0, 2, 0)))
    chosen((three, own), (jnp.where(here == 0, 0, 6), jnp.where(here == 0, 4, 2)))


def weights_body(embed, edge, proc, dec, out, padded):
    copies, width, columns = out.shape
    eye = one_hot(
        positions((width, width), 0), lax.broadcasted_iota(jnp.int32, (width, width), 1)
    )
    padded[...] = jnp.zeros_like(padded)
    padded[0 : embed.shape[0], :] = embed[...]
    at = 0
    for piece in (padded, edge, proc, dec):
        turned = mul_nt(eye, piece[...]).astype(BF16)
        for i in range(copies):
            out[i, :, at : at + piece.shape[0]] = turned
        at += piece.shape[0]


def tables_body(core, edges, *tables):
    is_even = core[0] == 0
    rows = edges.shape[1]
    order = (
        3,
        jnp.where(is_even, 4, 2),
        jnp.where(is_even, 5, 1),
        jnp.where(is_even, 1, 5),
        jnp.where(is_even, 0, 6),
        jnp.where(is_even, 2, 4),
        jnp.where(is_even, 6, 0),
    )
    count = edges.shape[0]
    spare = jnp.zeros((8 - count, rows), jnp.int32)
    ids = jnp.concatenate([edges[...], spare], axis=0).T
    nodes = sum(table.shape[1] for table in tables) // len(order)
    step = 128
    columns = positions((step, step), 1)
    for first in range(0, rows, step):
        wide = [
            jnp.broadcast_to(ids[first : first + step, k : k + 1], (step, step))
            for k in range(count)
        ]
        at = 0
        for table in tables:
            for block in range(table.shape[1] // nodes):
                base = order[at] * nodes
                moved = [(w - base).astype(jnp.int16) for w in wide]
                at += 1
                for part in range(0, nodes, step):
                    here = columns + jnp.int16(part)
                    total = one_hot(here, moved[0])
                    for k in range(1, count):
                        total += one_hot(here, moved[k])
                    left = block * nodes + part
                    table[first : first + step, left : left + step] = total


def messages(blocks, w_embed, w_edge, rows, sent):
    slots = blocks[0].shape[1]
    for i, block in enumerate(blocks):
        rows[:, i * slots : (i + 1) * slots] = silu_rows(w_embed, block)
    for i in range(len(blocks)):
        at = slice(i * slots, (i + 1) * slots)
        sent[:, at] = silu_rows(w_edge, rows[:, at])


def receivers(recv, offsets, hot):
    nodes, slots = hot.shape[0], recv.shape[-1]
    node_of = positions((nodes, slots), 0)
    for i, offset in enumerate(offsets):
        hot[:, i * slots : (i + 1) * slots] = one_hot(node_of, recv[offset])


def early_body(
    core, x, pack, up, down, three, weights, recv, embed, out, rows, sent, hot, padded, near, arrived
):
    is_even = core[0] == 0
    nodes, channels = embed.shape
    fetch = pltpu.make_async_copy(embed, near, arrived)
    fetch.start()
    slots = recv.shape[-1]
    w_embed = weights[:, 0:SENT]
    w_edge = weights[:, WIDE : WIDE + channels]
    padded[...] = jnp.zeros_like(padded)
    padded[0 : x.shape[0], :] = x[...]
    local = mul(padded[...], one_hot(positions((x.shape[1], slots), 0), pack[3])).astype(BF16)
    messages((local, up[0], down[0], three[...]), w_embed, w_edge, rows, sent)
    receivers(recv, (3, 5, 1, jnp.where(is_even, 6, 0)), hot)
    total = mul_nt(hot[...], sent[...])
    fetch.wait()
    out[...] = near[...].astype(F32) + total


def encode_body(
    core, here, early, sib, weights, recv, far_ids, latent, message, far, rows, sent, hot, w_proc
):
    is_even = core[0] == 0
    nodes, channels = early.shape
    w_embed = weights[:, 0:SENT]
    w_edge = weights[:, WIDE : WIDE + channels]
    w_proc[...] = weights[:, WIDE + channels : WIDE + 2 * channels]
    messages((sib[0], sib[1], sib[2]), w_embed, w_edge, rows, sent)
    offsets = (jnp.where(is_even, 2, 4), jnp.where(is_even, 4, 6), jnp.where(is_even, 0, 2))
    receivers(recv, offsets, hot)
    rounded = (early[...] + mul_nt(hot[...], sent[...])).astype(BF16)
    latent[...] = rounded
    made = silu(mul_nt(rounded, w_proc[...])).astype(BF16)
    message[...] = made
    far[...] = mul(far_table(far_ids, here[0], 1, nodes), made).astype(BF16)


def far_table(ids, here, sign, nodes):
    count = ids.shape[1]
    column = lax.broadcasted_iota(jnp.int32, ids.shape, 1)
    node = lax.broadcasted_iota(jnp.int32, (ids.shape[0], nodes), 1)
    pieces = []
    for offset in sum(FAR, ()):
        if offset is None:
            pieces.append(jnp.zeros((ids.shape[0], nodes), F32))
            continue
        partner = lax.rem(here + sign * offset + count, count)
        chosen = jnp.sum(jnp.where(column == partner, ids[...], 0), axis=1, keepdims=True)
        pieces.append(jnp.where(node == chosen, 1.0, 0.0))
    return jnp.concatenate(pieces, axis=0).astype(BF16)


def own_body(weights, x, block, table, out, padded):
    channels = x.shape[0]
    padded[...] = jnp.zeros_like(padded)
    padded[0:channels, :] = x[...]
    grid = silu(
        lax.dot_general(
            padded[...], weights[:, 0:WIDE], (((0,), (1,)), ((), ())), preferred_element_type=F32
        )
    ).astype(BF16)
    out[...] = grid.astype(F32) + mul(table[...], block[...])


def local_body(latent, message, neighbours, out):
    nodes = latent.shape[0]
    count = neighbours.shape[0]
    spare = jnp.zeros((8 - count, nodes), jnp.int32)
    ids = jnp.concatenate([neighbours[...], spare], axis=0).T
    node = lax.broadcasted_iota(jnp.int32, (nodes, nodes), 1)
    table = jnp.where(node == ids[:, 0:1], 1.0, 0.0)
    for k in range(1, count):
        table += jnp.where(node == ids[:, k : k + 1], 1.0, 0.0)
    out[...] = latent[...].astype(F32) + mul(table.astype(BF16), message[...])


def decode_body(here, base, far_ids, arrived, weights, out):
    nodes, channels = base.shape
    w_dec = weights[:, WIDE + 2 * channels :]
    hot = far_table(far_ids, here[0], -1, nodes)
    after = (base[...] + mul_tn(hot, arrived[...])).astype(BF16)
    out[...] = silu(mul_nt(after, w_dec)).astype(BF16)


def add_body(before, *rest):
    *blocks, table, out, joined = rest
    nodes = blocks[0].shape[0]
    for i, block in enumerate(blocks):
        joined[i * nodes : (i + 1) * nodes, :] = block[...]
    out[...] = before[...] + mul(table[...], joined[...])


def collect_body(before, *rest):
    *blocks, table, out, joined, done, left = rest
    nodes = blocks[0].shape[0]
    for i, block in enumerate(blocks):
        joined[i * nodes : (i + 1) * nodes, :] = block[...]
    step = out.shape[0] // 4
    stores = []
    for i in range(4):
        at = pl.ds(i * step, step)
        done[at, :] = (before[at, :] + mul(table[at, :], joined[...])).astype(BF16)
        stores.append(pltpu.make_async_copy(done.at[at, :], out.at[at, :], left.at[i]))
        stores[-1].start()
    for store in stores:
        store.wait()


def call(body, out_shape, args, scratch=(), name=None, stored=(), far_off=(), keeps=0):
    near = len(args)
    last = near + len(stored)
    args = (*args, *stored, *far_off)
    hbm = pl.BlockSpec(memory_space=pltpu.HBM)
    smem = pl.BlockSpec(memory_space=pltpu.SMEM)
    vmem = pl.BlockSpec(memory_space=pltpu.VMEM)
    many = isinstance(out_shape, (list, tuple))
    args = [
        a if a.ndim == 1 else pltpu.with_memory_space_constraint(a, place)
        for a, place in zip(args, [pltpu.VMEM] * near + [pltpu.HBM] * (len(args) - near))
    ]
    return pl.pallas_call(
        body,
        out_shape=out_shape,
        in_specs=[
            smem if a.ndim == 1 else hbm if i >= last else vmem for i, a in enumerate(args)
        ],
        out_specs=[vmem for _ in out_shape] if many else hbm if keeps else vmem,
        scratch_shapes=scratch,
        compiler_params=VMEM,
        name=name,
    )(*args)


def shape(*dims, kind=BF16):
    return pltpu.VMEM(dims, kind)


def far_exchange(rows, beside):
    patches, chans = lax.axis_size("patch"), lax.axis_size("chan")
    kinds = len(FAR[0])
    count, channels = rows.shape
    each = count // (chans * kinds)
    mine = lax.all_to_all(
        rows.reshape(chans, kinds * each, channels), "chan", 0, 0, tiled=True
    ).reshape(chans, kinds, each, channels)
    mine, beside = lax.optimization_barrier((mine, beside))
    arrived = []
    for kind in range(kinds):
        pairs = []
        for c in range(chans):
            if FAR[c][kind] is None:
                continue
            for p in range(patches):
                pairs.append((p * chans + c, (p + FAR[c][kind]) % patches * chans + c))
        arrived.append(lax.ppermute(mine[:, kind], ("patch", "chan"), pairs))
    back = jnp.stack(arrived, axis=1).reshape(chans, kinds * each, channels)
    return lax.all_to_all(back, "chan", 0, 0, tiled=True).reshape(count, channels), beside


def shards(
    grid_in,
    mesh_embed,
    w_embed,
    w_edge,
    w_proc,
    w_dec,
    pack_rows,
    recv_node,
    far_send,
    far_recv,
    loc_nbr,
    dec_edge,
):
    patch = lax.axis_index("patch").astype(jnp.int32)
    here = patch.reshape(1)
    core = (patch % 2).reshape(1)
    channels = mesh_embed.shape[1]
    nodes = mesh_embed.shape[0]
    rows = grid_in.shape[0]
    offsets, slots = pack_rows.shape[2:]
    x = grid_in.T
    pack = pack_rows.reshape(offsets, 1, slots)
    recv = recv_node.reshape(offsets, 1, slots)
    far_out_ids = far_send.reshape(far_send.shape[2:]).T
    far_in_ids = far_recv.reshape(far_recv.shape[2:]).T
    def stored(*dims):
        return pltpu.HBM(dims, BF16)

    def work(blocks):
        wide = pltpu.VMEM((channels, blocks * slots), BF16)
        return wide, wide, pltpu.VMEM((nodes, blocks * slots), BF16)

    block = shape(SENT, slots)
    pair = shape(2, SENT, slots)
    padded = pltpu.VMEM((SENT, rows), BF16)

    width = w_edge.shape[1]
    chans = lax.axis_size("chan")
    copies = call(
        weights_body,
        stored(chans, width, WIDE + 3 * channels),
        (),
        [pltpu.VMEM((WIDE, width), BF16)],
        name="weights",
        stored=(w_embed, w_edge, w_proc, w_dec),
    )
    copies, x, edges = lax.optimization_barrier((copies, x, dec_edge.T))
    weights = lax.all_to_all(copies, "chan", 0, 0, tiled=True).reshape(chans * width, -1)
    three, up, down, own = call(
        pack_body,
        [block, pair, pair, block],
        (core, x, pack),
        [pltpu.VMEM((rows, 2 * slots), BF16)],
        name="pack",
    )
    three = by_core(three, -3, 3)
    up = shifted(up, 2)
    down = shifted(down, -2)
    own_table, near_table, late_table = call(
        tables_body,
        [stored(rows, n * nodes) for n in (1, 3, 3)],
        (core,),
        name="tables",
        stored=(edges,),
    )
    three, up, own_table = lax.optimization_barrier((three, up, own_table))
    up, down = lax.optimization_barrier((up, down))
    sib = by_core(jnp.stack([own, up[1], down[1]]), 1, -1)
    early = call(
        early_body,
        shape(nodes, channels, kind=F32),
        (core, x, pack, up, down, three, weights, recv),
        [*work(4), padded, pltpu.VMEM((nodes, channels), BF16), pltpu.SemaphoreType.DMA],
        name="early",
        far_off=(mesh_embed,),
    )
    mesh_latent, node_msg, far_sent = call(
        encode_body,
        [stored(nodes, channels), stored(nodes, channels), shape(8 * 16, channels)],
        (core, here, early, sib, weights, recv, far_out_ids),
        [*work(3), pltpu.VMEM((channels, channels), BF16)],
        name="encode",
    )
    base = call(
        local_body,
        shape(nodes, channels, kind=F32),
        (),
        name="short",
        stored=(mesh_latent, node_msg, loc_nbr.T),
    )
    arrived, base = far_exchange(far_sent, base)
    dec_msg = call(
        decode_body,
        shape(nodes, channels),
        (here, base, far_in_ids, arrived, weights),
        name="decode",
    )

    def added(name, before, blocks, table):
        return call(
            add_body,
            shape(rows, channels, kind=F32),
            (before, *blocks, table),
            [pltpu.VMEM((len(blocks) * nodes, channels), BF16)],
            name=name,
        )

    second = by_core(dec_msg, 2, -2)
    first = by_core(dec_msg, -2, 2)
    sib = by_core(dec_msg, 1, -1)
    total = call(
        own_body,
        shape(rows, channels, kind=F32),
        (weights, x, dec_msg, own_table),
        [pltpu.VMEM((WIDE, rows), BF16)],
        name="own",
    )
    first, total = lax.optimization_barrier((first, total))
    three = by_core(first, -1, 1)
    relay_first = by_core(first, 1, -1)
    relay_second = by_core(second, 1, -1)
    total = added("near", total, (sib, first, second), near_table)
    return call(
        collect_body,
        stored(rows, channels),
        (total, three, relay_first, relay_second, late_table),
        [
            pltpu.VMEM((3 * nodes, channels), BF16),
            pltpu.VMEM((rows, channels), BF16),
            pltpu.SemaphoreType.DMA((4,)),
        ],
        name="collect",
        keeps=1,
    )


def solution(mesh):
    both = P(("patch", "chan"), None)
    column = P(None, "chan")
    lists = P("patch", "chan", None, None)
    in_specs = (both, both, column, column, column, column, lists, lists, lists, lists, both, both)
    return jax.shard_map(shards, mesh=mesh, in_specs=in_specs, out_specs=both, check_vma=False)
```
